32 devices in a mesh: slab: 16 (over z, x, core), view: 2 (over y).
Axes of the slice: x: 2, y: 2, z: 4, core: 2. Of those that a mesh axis runs over, the one named last changes fastest.
Arguments:
- activity: float32 [512, 32, 1024], P('slab'), may hold values from 0.5 to 2
- sensitivity: float32 [512, 32, 1024], P('slab'), may hold values from 1 to 8
- psf_width: float32 [512], P('slab'), may hold values from 0.05 to 0.3
- measured: bfloat16 [2, 1024, 32, 128], P('view', 'slab'), may hold values from 0.25 to 4
- block_slab: int32 [2, 1024, 1], P('view', 'slab'), may hold values from 0 to 15; in each aligned block of 64 rows (0 to 63, 64 to 127, ..., all dimensions but the last counted through in order) at most 8 rows name the same one
- block_line: int32 [2, 1024], P('view', 'slab'), may hold values from 0 to 31
- block_angle: int32 [2, 1024], P('view', 'slab'), may hold values from 0 to 7
- subset_views: int32 [2, 8], P('view'), may hold values from 0 to 335
Outputs:
- updated: float32 [512, 32, 1024], P('slab')
The draws below stay inside these ranges and needn't reach their ends.
Inputs may be any that keep to these rules, and one draw needn't show every extreme that they name: `block_slab`: among the 64 blocks of one device (aligned blocks of 64 rows) no slab is named more than 8 times, a bound that some block reaches.
All inputs are finite; a program needn't handle non-finite values.
Results may differ from the reference program's by a relative error of at most 0.0014.
Values may be sent and summed in bfloat16 or wider, within the bound.
No kernel may reach another device: no remote copies, remote signals or barrier semaphores. Data moves between devices by JAX's collectives and lax.ppermute only.
A program may use at most 64 MiB of HBM per device.

```python
import math
import jax
import jax.numpy as jnp
import numpy as np
from jax import lax

ZS = 32
LINES = 32
VL = 1024
BINS = 128
ANG = 8
VIEWS_ALL = 336
NB = 64
Z = 512
BLOCKS = 1024
CAP = 8
N_SLAB = 16
N_VIEW = 2


def touch_ends(drawn, own_key, least, high):
    longest = drawn.shape.index(max(drawn.shape))
    spots = []
    for shift in (0, 1):
        where = [jax.random.randint(jax.random.fold_in(own_key, axis), (), 0, length) for axis, length in enumerate(drawn.shape)]
        where[longest] = (where[longest] + shift) % drawn.shape[longest]
        spots.append(tuple(where))
    return drawn.at[spots[0]].set(least).at[spots[1]].set(high)


def block_levels(own_key, shape, pieces, least, top_value):
    def one(axis_at, blocks):
        heights = jax.random.uniform(jax.random.fold_in(jax.random.fold_in(own_key, 6), axis_at), (blocks,), jnp.float32, least / len(pieces), top_value / len(pieces))
        return jnp.repeat(jnp.exp(heights), shape[axis_at] // blocks).reshape((-1,) + (1,) * (len(shape) - axis_at - 1))

    factor_of = one(*pieces[0])
    for cut in pieces[1:]:
        factor_of = factor_of * one(*cut)
    return factor_of


def deal_out(rng, own, number, rows, count, top, reach, slope):
    order = jax.random.permutation(rng, count)
    heavy_load, ordinary = portions_of(count, rows * top, reach, slope, True), portions_of(count, rows * top, reach, slope, False)
    places = jnp.arange(count)

    def named(sizes, turn):
        used = int((sizes > 0).sum())
        fixed = max(1, used // 4)
        passed = fixed + (places - fixed + turn * (used - fixed)) % max(1, count - fixed)
        return jnp.zeros((count,), jnp.int32).at[order[jnp.where(places < fixed, places, passed)]].set(jnp.asarray(sizes, jnp.int32))

    sizes = jnp.where(number % 4 == 0, named(heavy_load, number // 4), named(ordinary, number - number // 4 - 1))
    mixed = jax.random.permutation(jax.random.fold_in(own, 3), count)
    donor, taker = mixed[0:count // 2 * 2:2], mixed[1:count // 2 * 2:2]
    slack = jnp.minimum(sizes[donor] - 1, reach - sizes[taker]) // 2
    slack = jnp.where((donor == order[0]) | (taker == order[0]) | (sizes[taker] == 0), 0, jnp.maximum(slack, 0))
    passed = jax.random.randint(jax.random.fold_in(own, 4), (count // 2,), 0, 1 << 20) % (slack + 1)
    sizes = sizes.at[donor].add(-passed).at[taker].add(passed)
    labels = jnp.searchsorted(jnp.cumsum(sizes), jnp.arange(rows * top), side="right").astype(jnp.int32)
    listing = labels.reshape(top, rows).T
    listing = listing[jax.random.permutation(jax.random.fold_in(own, 1), rows)]
    turn = jax.random.randint(jax.random.fold_in(own, 2), (rows, 1), 0, top)
    return jnp.take_along_axis(listing, (jnp.arange(top)[None, :] + turn) % top, axis=1)


def portions_of(count, total, limit, lean, full):
    portions = [(1 << 20) // math.isqrt(standing ** lean) + 1 for standing in range(1, count + 1)]
    largest = limit if full else min(limit, max(-(-total // count), total * portions[0] // sum(portions)))
    least = 1 if total - largest >= count - 1 else 0
    counts, rest = [largest] + [least] * (count - 1), total - largest - least * (count - 1)
    while rest > 0:
        candidates = [i for i in range(1, count) if counts[i] < largest] or [i for i in range(1, count) if counts[i] < limit]
        mass, left = sum([portions[i] for i in candidates]), rest
        for i in candidates:
            extra = min(limit - counts[i], max(1, left * portions[i] // mass), rest)
            counts[i] = counts[i] + extra
            rest = rest - extra
    return np.array(counts)


def setup_inputs(seed: int = 0) -> dict:
    arg_keys = jax.random.split(jax.random.key(seed), 9)
    activity = jnp.clip(jnp.exp(math.log(2.0) - 1.3862944 * jax.random.uniform(arg_keys[0], (Z, LINES, VL), jnp.float32) ** block_levels(arg_keys[0], (Z, LINES, VL), ((0, 16),), -0.2, 0.2)), 0.5, 2.0)
    sensitivity = jnp.clip(jnp.exp(math.log(8.0) - 2.0794415 * jax.random.uniform(arg_keys[1], (Z, LINES, VL), jnp.float32) ** block_levels(arg_keys[1], (Z, LINES, VL), ((0, 16),), -0.2, 0.2)), 1.0, 8.0)
    psf_width = jnp.clip(0.05 + 0.25 * jax.random.uniform(arg_keys[2], (Z,), jnp.float32) ** block_levels(arg_keys[2], (Z,), ((0, 16),), -0.2, 0.2), 0.05, 0.3)
    measured = jnp.clip(jnp.exp(math.log(4.0) - 2.7725887 * jax.random.uniform(arg_keys[3], (N_VIEW, BLOCKS, ZS, BINS), jnp.float32) ** block_levels(arg_keys[3], (N_VIEW, BLOCKS, ZS, BINS), ((0, 2), (1, 16)), -0.2, 0.2)), 0.25, 4.0).astype(jnp.bfloat16)
    block_slab_keys = jax.random.split(jax.random.fold_in(arg_keys[4], 1), N_VIEW * BLOCKS // NB)
    block_slab_turns = jax.random.permutation(jax.random.fold_in(arg_keys[4], 3), N_VIEW * BLOCKS // NB)
    block_slab = jax.vmap(lambda own, number: deal_out(jax.random.fold_in(arg_keys[4], 2), own, number, NB, N_SLAB, 1, CAP, 2))(block_slab_keys, block_slab_turns).reshape((N_VIEW, BLOCKS, 1))
    block_line = touch_ends(jax.random.randint(arg_keys[5], (N_VIEW, BLOCKS), 0, LINES), jax.random.fold_in(arg_keys[5], 1), 0, LINES - 1).astype(jnp.int32)
    block_angle = touch_ends(jax.random.randint(arg_keys[6], (N_VIEW, BLOCKS), 0, ANG), jax.random.fold_in(arg_keys[6], 1), 0, ANG - 1).astype(jnp.int32)
    subset_views = touch_ends(jax.random.randint(arg_keys[7], (N_VIEW, ANG), 0, VIEWS_ALL), jax.random.fold_in(arg_keys[7], 1), 0, VIEWS_ALL - 1).astype(jnp.int32)
    return {"activity": activity, "sensitivity": sensitivity, "psf_width": psf_width, "measured": measured, "block_slab": block_slab, "block_line": block_line, "block_angle": block_angle, "subset_views": subset_views}


BACKGROUND = 0.05

def kernels(angles, bins, length):
    view_angle = math.pi * angles.astype(jnp.float32) / VIEWS_ALL
    step_width = length / bins
    deviation = 0.25 * step_width
    spacing = step_width * (0.75 + 0.25 * jnp.cos(2.0 * view_angle))
    offset = 1.5 * step_width * jnp.sin(view_angle)
    centres = (jnp.arange(bins, dtype=jnp.float32) + 0.5 - bins / 2)[None, :] * spacing[:, None] + offset[:, None]
    voxel_pos = jnp.arange(length, dtype=jnp.float32) + 0.5 - length / 2
    distance = voxel_pos[None, None, :] - centres[:, :, None]
    values = jnp.exp(-distance * distance / (2.0 * deviation * deviation)) / (deviation * math.sqrt(2.0 * math.pi))
    return values.astype(jnp.bfloat16)

def blur_forward(field, weight):
    padded = jnp.pad(field, ((1, 1), (0, 0), (0, 0)))
    wide = weight[:, None, None]
    return (1.0 - 2.0 * wide) * field + wide * (padded[:-2] + padded[2:])

def blur_adjoint(field, weight):
    wide = weight[:, None, None]
    padded = jnp.pad(wide * field, ((1, 1), (0, 0), (0, 0)))
    return (1.0 - 2.0 * wide) * field + padded[:-2] + padded[2:]

def reference(activity, sensitivity, psf_width, measured, block_slab, block_line, block_angle, subset_views):
    blurred = blur_forward(activity, psf_width).astype(jnp.bfloat16)
    planes = blurred.reshape(N_SLAB, ZS, LINES, VL)
    total = jnp.zeros((N_SLAB, ZS, LINES, VL), jnp.float32)
    for group in range(N_VIEW):
        tof_kernel = kernels(subset_views[group], BINS, VL)
        targets = block_slab[group, :, 0]
        line_ids = block_line[group]
        angle_ids = block_angle[group]

        def project(packed):
            slab_ids, line_part, angle_part = packed
            tiles = planes[slab_ids, :, line_part, :]
            chosen = tof_kernel[angle_part]
            return jnp.einsum('bzv,btv->bzt', tiles.astype(jnp.float32), chosen.astype(jnp.float32))
        estimate = lax.map(project, (targets.reshape(-1, 32), line_ids.reshape(-1, 32), angle_ids.reshape(-1, 32)))
        estimate = estimate.reshape(BLOCKS, ZS, BINS)
        ratios = measured[group].astype(jnp.float32) / (estimate + BACKGROUND)
        segment = (targets * ANG + angle_ids) * LINES + line_ids
        sums = jax.ops.segment_sum(ratios, segment, num_segments=N_SLAB * ANG * LINES)
        rounded = sums.astype(jnp.bfloat16).reshape(N_SLAB, ANG, LINES, ZS, BINS)
        total = total + jnp.einsum('salzt,atv->szlv', rounded.astype(jnp.float32), tof_kernel.astype(jnp.float32))
    smoothed = blur_adjoint(total.reshape(Z, LINES, VL), psf_width)
    return activity * smoothed / sensitivity
```

```python
import functools
import math

import jax
import jax.numpy as jnp
from jax import lax
from jax.experimental import pallas as pl
from jax.experimental.pallas import tpu as pltpu
from jax.sharding import PartitionSpec as P

VIEWS_ALL = 336
BACKGROUND = 0.05
SLOTS = 8
EDGE = 2 * SLOTS
META = 16
HALF = 64
F32 = jnp.float32
BF16 = jnp.bfloat16
SMEM = pltpu.SMEM
VMEM = pltpu.VMEM
MIB = 1024 * 1024


def iota(shape, dim):
    return lax.broadcasted_iota(jnp.int32, shape, dim)


def matmul(a, b, contract=(1, 0)):
    dims = (((contract[0],), (contract[1],)), ((), ()))
    return lax.dot_general(a, b, dims, preferred_element_type=F32)


def params(limit):
    return pltpu.CompilerParams(vmem_limit_bytes=limit * MIB)


def bucket_kernel(
    slabs, capacity, lines, slab_s, slab_v, line_v, angle_v, measured, out, count, extra, sems
):
    blocks, planes, bins = measured.shape
    body = capacity * planes
    for s in range(slabs):
        count[s] = 0

    def send(m, carry):
        s = slab_s[0, m]
        place = count[s]
        count[s] = place + 1
        start = pl.multiple_of(place * planes, planes)
        pltpu.make_async_copy(
            measured.at[m], out.at[s, pl.ds(start, planes), :], sems.at[0]
        ).start()
        return carry

    lax.fori_loop(0, blocks, send, 0)

    slab = slab_v[...]
    code = (angle_v[...] * lines + line_v[...] + 1).astype(F32)
    names = (iota((slabs, blocks), 0) == slab).astype(F32)
    earlier = (iota((blocks, blocks), 0) < iota((blocks, blocks), 1)).astype(BF16)
    ranks = matmul(names.astype(BF16), earlier)
    slot = jnp.sum(names * ranks, axis=0, keepdims=True).astype(jnp.int32)

    row = iota((slabs * EDGE, blocks), 0)
    place = row % EDGE
    before = place < SLOTS
    wanted = jnp.where(before, row // EDGE - 1, row // EDGE + 1)
    match = (slab == wanted) & (slot == place % SLOTS)
    chosen = match.astype(F32).astype(BF16)
    chosen_last = (match & before).astype(F32).astype(BF16)
    chosen_first = (match & ~before).astype(F32).astype(BF16)
    flat = measured[...].reshape(blocks * planes, bins)
    column = iota((blocks, blocks * planes), 1)
    base = iota((blocks, blocks * planes), 0) * planes
    first_rows = matmul((column == base).astype(F32).astype(BF16), flat).astype(BF16)
    last_rows = matmul((column == base + planes - 1).astype(F32).astype(BF16), flat).astype(BF16)
    edges = matmul(chosen_last, last_rows) + matmul(chosen_first, first_rows)
    extra[:, 0:EDGE, :] = edges.astype(BF16).reshape(slabs, EDGE, bins)

    lane = iota((bins, blocks), 0)
    low = jnp.where(lane < HALF, code, 0.0).astype(BF16)
    edge_codes = matmul(chosen, low, (1, 1)).reshape(slabs, EDGE, bins)
    own_slot = (slot + HALF == lane).astype(F32).astype(BF16)
    own_codes = matmul((names * code).astype(BF16), own_slot, (1, 1))
    extra[:, EDGE:, :] = (edge_codes + own_codes.reshape(slabs, 1, bins)).astype(BF16)

    tail = pltpu.make_async_copy(extra, out.at[:, pl.ds(body, EDGE + META), :], sems.at[1])
    tail.start()
    pltpu.make_async_copy(measured, measured, sems.at[0]).wait()
    tail.wait()


def bucket(measured, slab, line, angle, slabs, capacity, lines):
    blocks, planes, bins = measured.shape
    rows = capacity * planes + EDGE + META
    vmem = pl.BlockSpec(memory_space=VMEM)
    return pl.pallas_call(
        functools.partial(bucket_kernel, slabs, capacity, lines),
        out_shape=jax.ShapeDtypeStruct((slabs, rows, bins), BF16),
        in_specs=[pl.BlockSpec(memory_space=SMEM)] + [vmem] * 4,
        out_specs=pl.BlockSpec(memory_space=pl.ANY),
        scratch_shapes=[
            SMEM((slabs,), jnp.int32),
            VMEM((slabs, EDGE + META, bins), BF16),
            pltpu.SemaphoreType.DMA((2,)),
        ],
        compiler_params=params(16),
        name="bucket",
    )(slab, slab, line, angle, measured)


def front_kernel(groups, lines, width, spacing, offset, activity, low, high, k_out, r_out, blurred):
    rows, length = activity.shape
    planes = rows // lines
    angles = spacing.shape[1]
    bins = k_out.shape[1] // angles

    def put(at, w, here, down, up):
        value = (1.0 - 2.0 * w) * here + w * (down + up)
        blurred[pl.ds(at, lines), :] = value.astype(BF16)

    def plane(z):
        return activity[pl.ds(z * lines, lines), :]

    near_low, near_high = low[lines : 2 * lines, :], high[0:lines, :]
    wide_low = low[2 * lines : 2 * lines + 1, :]
    wide_high = high[2 * lines : 2 * lines + 1, :]
    put(0, wide_low, near_low, low[0:lines, :], plane(0))
    put(lines, width[0], plane(0), near_low, plane(1))
    put(planes * lines, width[planes - 1], plane(planes - 1), plane(planes - 2), near_high)
    put((planes + 1) * lines, wide_high, near_high, plane(planes - 1), high[lines : 2 * lines, :])

    def inner(z, carry):
        start = pl.multiple_of(z * lines, lines)
        here = activity[pl.ds(start, lines), :]
        down = activity[pl.ds(pl.multiple_of(start - lines, lines), lines), :]
        up = activity[pl.ds(pl.multiple_of(start + lines, lines), lines), :]
        put(pl.multiple_of(start + lines, lines), width[z], here, down, up)
        return carry

    lax.fori_loop(1, planes - 1, inner, 0)

    step_width = length / bins
    deviation = 0.25 * step_width
    scale = deviation * math.sqrt(2.0 * math.pi)
    some = 16
    chunk = r_out.shape[1] // 4
    for g in range(groups):

        def fill(i, carry, g=g):
            start = pl.multiple_of(i * some, some)
            a = i // (bins // some)
            first = (i % (bins // some)) * some
            t = (iota((some, length), 0) + first).astype(F32) + 0.5 - bins / 2
            voxel = iota((some, length), 1).astype(F32) + 0.5 - length / 2
            distance = voxel - (t * spacing[g, a] + offset[g, a])
            value = jnp.exp(-distance * distance / (2.0 * deviation * deviation)) / scale
            k_out[g, pl.ds(start, some), :] = value.astype(BF16)
            return carry

        lax.fori_loop(0, angles * bins // some, fill, 0)

        def project(i, carry, g=g):
            start = pl.multiple_of(i * chunk, 16)
            estimate = matmul(blurred[pl.ds(start, chunk), :], k_out[g], (1, 1))
            r_out[g, pl.ds(start, chunk), :] = 1.0 / (estimate + BACKGROUND)
            return carry

        lax.fori_loop(0, 4, project, 0)


def front(width, spacing, offset, activity, low, high, lines, bins):
    rows, length = activity.shape
    groups, angles = spacing.shape
    extended = rows + 2 * lines
    smem, vmem = pl.BlockSpec(memory_space=SMEM), pl.BlockSpec(memory_space=VMEM)
    flops = groups * 2 * extended * length * angles * bins
    return pl.pallas_call(
        functools.partial(front_kernel, groups, lines),
        out_shape=(
            jax.ShapeDtypeStruct((groups, angles * bins, length), BF16),
            jax.ShapeDtypeStruct((groups, extended, angles * bins), F32),
        ),
        in_specs=[smem, smem, smem, vmem, vmem, vmem],
        out_specs=(vmem, vmem),
        scratch_shapes=[VMEM((extended, length), BF16)],
        compiler_params=params(48),
        cost_estimate=pl.CostEstimate(
            flops=flops, bytes_accessed=rows * length * 12, transcendentals=groups * MIB
        ),
        name="front",
    )(width, spacing, offset, activity, low, high)


def tail_kernel(
    capacity, lines, *refs
):
    (width, low, high, received, k_in, r_in, activity_in, sensitivity_in, out) = refs[:9]
    (sums, total, k_buf, r_buf, activity, sensitivity, updated, codes_v, codes, sems) = refs[9:]
    groups, slabs, rows_sent, bins = received.shape
    rows, length = activity.shape
    planes = rows // lines
    extended = rows + 2 * lines
    angles = k_in.shape[1] // bins
    body = capacity * planes
    shift = lines.bit_length() - 1

    def fetch(g):
        slot = g % 2
        return (
            pltpu.make_async_copy(k_in.at[g], k_buf.at[slot], sems.at[slot]),
            pltpu.make_async_copy(r_in.at[g], r_buf.at[slot], sems.at[2 + slot]),
        )

    for copy in fetch(0):
        copy.start()
    for g in range(groups):
        for s in range(slabs):
            tile = received[g, s, body + EDGE : body + EDGE + META, :].astype(F32)
            codes_v[g * slabs + s : g * slabs + s + 1, :] = tile[0:1, :].astype(jnp.int32)
    list_codes = pltpu.make_async_copy(codes_v, codes, sems.at[4])
    list_codes.start()
    get_activity = pltpu.make_async_copy(activity_in, activity, sems.at[5])
    get_activity.start()
    get_sensitivity = pltpu.make_async_copy(sensitivity_in, sensitivity, sems.at[6])
    get_sensitivity.start()

    chunk = extended // 4
    for g in range(groups):
        if g + 1 < groups:
            for copy in fetch(g + 1):
                copy.start()

        def clear(i, carry):
            start = pl.multiple_of(lines + i * lines, lines)
            for a in range(angles):
                sums[a, pl.ds(start, lines), :] = jnp.zeros((lines, bins), F32)
            return carry

        lax.fori_loop(0, planes, clear, 0)

        side = slabs * SLOTS
        edge_rows = received[g, :, body : body + EDGE, :].astype(F32)
        edge_codes = received[g, :, body + EDGE : body + EDGE + META, :].astype(F32)
        lane = iota((side, bins), 1)
        for part, at in ((0, 0), (1, extended - lines)):
            data = edge_rows[:, part * SLOTS : (part + 1) * SLOTS, :].reshape(side, bins)
            code = edge_codes[:, part * SLOTS : (part + 1) * SLOTS, :].reshape(side, bins)
            code = jnp.where(lane < HALF, code, pltpu.roll(code, HALF, 1)).astype(jnp.int32)
            index = code - 1
            named = (index & (lines - 1) == lane) & (code > 0)
            named = jnp.transpose(named.astype(F32))[0:lines, :].astype(BF16)
            for a in range(angles):
                of_angle = (index >> shift == a) & (code > 0)
                spread = jnp.where(of_angle, data, 0.0).astype(BF16)
                sums[a, at : at + lines, :] = matmul(named, spread)

        if g == 0:
            list_codes.wait()

        def scatter(s, carry, g=g):
            for p in range(capacity):
                code = codes[g * slabs + s, HALF + p]

                @pl.when(code > 0)
                def _():
                    index = code - 1
                    a = index >> shift
                    place = pl.ds(lines + (index & (lines - 1)), planes, stride=lines)
                    block = received[g, s, p * planes : (p + 1) * planes, :].astype(F32)
                    sums[a, place, :] = sums[a, place, :] + block

            return carry

        lax.fori_loop(0, slabs, scatter, 0)

        for copy in fetch(g):
            copy.wait()

        def project(i, carry, g=g):
            start = pl.multiple_of(i * chunk, 16)
            here = pl.ds(start, chunk)
            parts = []
            for a in range(angles):
                inverse = r_buf[g % 2, here, a * bins : (a + 1) * bins]
                parts.append((sums[a, here, :] * inverse).astype(BF16))
            back = matmul(jnp.concatenate(parts, axis=1), k_buf[g % 2])
            total[here, :] = back if g == 0 else total[here, :] + back
            return carry

        lax.fori_loop(0, 4, project, 0)

    get_activity.wait()
    get_sensitivity.wait()
    wide_low, wide_high = low[0:1, :], high[0:1, :]

    def smooth(z, w_down, w_up):
        start = z * lines
        w = width[z]
        down = total[pl.ds(start, lines), :]
        here = total[pl.ds(start + lines, lines), :]
        up = total[pl.ds(start + 2 * lines, lines), :]
        smoothed = (1.0 - 2.0 * w) * here + w_down * down + w_up * up
        at = pl.ds(start, lines)
        updated[at, :] = activity[at, :] * smoothed / sensitivity[at, :]

    pieces = 4
    count = planes // pieces
    writes = []
    for piece in range(pieces):
        first, last = piece * count, (piece + 1) * count
        if piece == 0:
            smooth(0, wide_low, width[1])
            first = 1
        if piece == pieces - 1:
            last = planes - 1

        def inner(z, carry):
            smooth(z, width[z - 1], width[z + 1])
            return carry

        lax.fori_loop(first, last, inner, 0)
        if piece == pieces - 1:
            smooth(planes - 1, width[planes - 2], wide_high)
        at = pl.ds(piece * count * lines, count * lines)
        write = pltpu.make_async_copy(updated.at[at, :], out.at[at, :], sems.at[7 + piece])
        write.start()
        writes.append(write)
    for write in writes:
        write.wait()


def tail(width, low, high, received, k_all, r_all, activity, sensitivity, capacity, lines):
    groups, slabs, _, bins = received.shape
    rows, length = activity.shape
    extended = rows + 2 * lines
    wide = k_all.shape[1]
    angles = wide // bins
    smem, vmem = pl.BlockSpec(memory_space=SMEM), pl.BlockSpec(memory_space=VMEM)
    anywhere = pl.BlockSpec(memory_space=pl.ANY)
    edge = pl.BlockSpec((8, length), lambda i: (2 * lines // 8, 0))
    whole = pl.BlockSpec(received.shape, lambda i: (0, 0, 0, 0))
    return pl.pallas_call(
        functools.partial(tail_kernel, capacity, lines),
        out_shape=jax.ShapeDtypeStruct((rows, length), F32),
        grid=(1,),
        in_specs=[smem, edge, edge, whole] + [anywhere] * 4,
        out_specs=anywhere,
        scratch_shapes=[
            VMEM((angles, extended, bins), F32),
            VMEM((extended, length), F32),
            VMEM((2, wide, length), BF16),
            VMEM((2, extended, wide), F32),
            VMEM((rows, length), F32),
            VMEM((rows, length), F32),
            VMEM((rows, length), F32),
            VMEM((groups * slabs, bins), jnp.int32),
            SMEM((groups * slabs, bins), jnp.int32),
            pltpu.SemaphoreType.DMA((11,)),
        ],
        compiler_params=params(56),
        cost_estimate=pl.CostEstimate(
            flops=groups * 2 * extended * length * wide,
            bytes_accessed=rows * length * 12,
            transcendentals=0,
        ),
        name="tail",
    )(width, low, high, received, k_all, r_all, activity, sensitivity)


def other_groups(value):
    size = lax.axis_size("view")
    if size == 2:
        other = lax.ppermute(value, "view", [(0, 1), (1, 0)])
        return jnp.stack([value, other])
    return lax.all_gather(value, "view")


def on_device(
    activity, sensitivity, psf_width, measured, block_slab, block_line, block_angle, subset_views
):
    planes, lines, length = activity.shape
    _, blocks, _, bins = measured.shape
    slabs = lax.axis_size("slab")
    capacity = 2 * blocks // slabs
    assert capacity <= SLOTS and subset_views.shape[1] * lines <= 256

    flat = activity.reshape(planes * lines, length)
    ups = [(i, i + 1) for i in range(slabs - 1)]
    downs = [(j, i) for i, j in ups]
    wide_first = jnp.broadcast_to(psf_width[0:1, None], (8, length))
    wide_last = jnp.broadcast_to(psf_width[planes - 1 :, None], (8, length))
    low = lax.ppermute(jnp.concatenate([flat[-2 * lines :], wide_last]), "slab", ups)
    high = lax.ppermute(jnp.concatenate([flat[: 2 * lines], wide_first]), "slab", downs)

    views = other_groups(subset_views[0])
    angle = math.pi * views.astype(F32) / VIEWS_ALL
    step_width = length / bins
    spacing = step_width * (0.75 + 0.25 * jnp.cos(2.0 * angle))
    offset = 1.5 * step_width * jnp.sin(angle)

    send = bucket(
        measured[0], block_slab.reshape(1, blocks), block_line, block_angle, slabs, capacity, lines
    )
    own = lax.all_to_all(send, "slab", split_axis=0, concat_axis=0, tiled=True)
    received = other_groups(own)

    k_all, r_all = front(psf_width, spacing, offset, flat, low, high, lines, bins)
    result = tail(
        psf_width,
        low,
        high,
        received,
        k_all,
        r_all,
        flat,
        sensitivity.reshape(planes * lines, length),
        capacity,
        lines,
    )
    return result.reshape(planes, lines, length)


def solution(mesh):
    in_specs = (
        P("slab", None, None),
        P("slab", None, None),
        P("slab"),
        P("view", "slab", None, None),
        P("view", "slab", None),
        P("view", "slab"),
        P("view", "slab"),
        P("view", None),
    )
    out_specs = P("slab", None, None)
    return jax.shard_map(
        on_device, mesh=mesh, in_specs=in_specs, out_specs=out_specs, check_vma=False
    )
```

```python
import functools
import math

import jax
import jax.numpy as jnp
from jax import lax
from jax.experimental import pallas as pl
from jax.experimental.pallas import tpu as pltpu
from jax.sharding import PartitionSpec as P

VIEWS_ALL = 336
BACKGROUND = 0.05
SLOTS = 8
PAIR = 2 * SLOTS
META = 16
WIDE = 64
F32 = jnp.float32
BF16 = jnp.bfloat16
I32 = jnp.int32
SMEM = pltpu.SMEM
VMEM = pltpu.VMEM
MIB = 1024 * 1024
LIMIT_FRONT = 12
LIMIT_BACK = 14
LIMIT_UPDATE = 16


def iota(shape, dim):
    return lax.broadcasted_iota(I32, shape, dim)


def matmul(a, b, contract=(1, 0)):
    dims = (((contract[0],), (contract[1],)), ((), ()))
    return lax.dot_general(a, b, dims, preferred_element_type=F32)


def params(limit):
    return pltpu.CompilerParams(vmem_limit_bytes=limit * MIB)


def cost(flops, moved):
    return pl.CostEstimate(flops=flops, bytes_accessed=moved, transcendentals=0)


SPEC_SMEM = pl.BlockSpec(memory_space=SMEM)
SPEC_VMEM = pl.BlockSpec(memory_space=VMEM)
SPEC_ANY = pl.BlockSpec(memory_space=pl.ANY)
SPEC_HBM = pl.BlockSpec(memory_space=pltpu.HBM)


def one_hot(mask):
    return mask.astype(F32).astype(BF16)


def bucket_kernel(chips, relative, planes, lines, *refs):
    raws, tables = refs[0:2], refs[2:4]
    out, wide, flat = refs[4:]
    rows, bins = raws[0].shape
    blocks = rows // planes
    both = 2 * blocks
    me = lax.axis_index("slab")

    for i, raw in enumerate(raws):
        wide[i] = raw[...].astype(F32)

    def turn(z, carry):
        column = pl.ds(pl.multiple_of(z * bins, bins), bins)
        for i in range(2):
            part = wide[i, pl.ds(z, blocks, stride=planes), :]
            flat[i * blocks : (i + 1) * blocks, column] = part.astype(BF16)
        return carry

    lax.fori_loop(0, planes, turn, 0, unroll=4)

    def lanes(row):
        return tables[0][row : row + 1, :] + pltpu.roll(tables[1][row : row + 1, :], blocks, 1)

    slab, code = lanes(0), (lanes(2) * lines + lanes(1) + 1).astype(F32)
    shape = (both, both)
    earlier = (iota(shape, 0) < iota(shape, 1)) & (iota(shape, 0) // blocks == iota(shape, 1) // blocks)
    names = (iota((WIDE, both), 0) == slab).astype(F32)
    ranks = matmul(names.astype(BF16), one_hot(earlier))
    slot = jnp.sum(names * ranks, axis=0, keepdims=True).astype(I32)
    slot = slot + iota((1, both), 1) // blocks * SLOTS

    def target(chip):
        return (2 * chip) ^ me if relative else 2 * chip + (me & 1)

    row = iota((chips * PAIR, both), 0)
    aim = target(row // PAIR)
    here = slot == row % PAIR
    chosen = one_hot((slab == aim) & here)

    some = 2

    def deal(i, carry):
        column = pl.ds(pl.multiple_of(i * some * bins, some * bins), some * bins)
        dealt = matmul(chosen, flat[:, column]).astype(BF16)
        for j in range(some):
            at = pl.ds(pl.multiple_of((i * some + j) * PAIR, PAIR), PAIR)
            for chip in range(chips):
                part = dealt[chip * PAIR : (chip + 1) * PAIR, j * bins : (j + 1) * bins]
                out[chip, at, :] = part
        return carry

    lax.fori_loop(0, planes // some, deal, 0, unroll=4)

    body = planes * PAIR
    aim_row = target(iota((chips, both), 0))
    lane = iota((bins, both), 0)
    codes = jnp.zeros((chips, bins), F32)
    for kind, (shift, z) in enumerate(((0, None), (-1, planes - 1), (1, 0))):
        picked = ((slab == aim_row + shift).astype(F32) * code).astype(BF16)
        codes = codes + matmul(picked, one_hot(slot + kind * PAIR == lane), (1, 1))
        if kind:
            edge = one_hot((slab == aim + shift) & here)
            dealt = matmul(edge, flat[:, z * bins : (z + 1) * bins]).astype(BF16)
            at = body + (kind - 1) * PAIR
            for chip in range(chips):
                out[chip, at : at + PAIR, :] = dealt[chip * PAIR : (chip + 1) * PAIR, :]
    codes = codes.astype(BF16)
    for chip in range(chips):
        spread = jnp.broadcast_to(codes[chip : chip + 1, :].astype(F32), (META, bins))
        out[chip, body + 2 * PAIR :, :] = spread.astype(BF16)


def bucket(raws, tables, chips, relative, planes, lines):
    rows, bins = raws[0].shape
    sent = (planes + 2) * PAIR + META
    return pl.pallas_call(
        functools.partial(bucket_kernel, chips, relative, planes, lines),
        out_shape=jax.ShapeDtypeStruct((chips, sent, bins), BF16),
        in_specs=[SPEC_VMEM] * 4,
        out_specs=SPEC_VMEM,
        scratch_shapes=[VMEM((2, rows, bins), F32), VMEM((2 * rows // planes, planes * bins), BF16)],
        compiler_params=params(24),
        cost_estimate=cost(10**8, 4 * MIB),
        name="bucket",
    )(*raws, *tables)


def halo_kernel(width, first, final, low_out, high_out):
    edge, length = first.shape
    low_out[0:edge, :] = final[...]
    low_out[edge : edge + 8, :] = jnp.full((8, length), width[width.shape[0] - 1], F32)
    high_out[0:edge, :] = first[...]
    high_out[edge : edge + 8, :] = jnp.full((8, length), width[0], F32)


def halo(width, activity, lines):
    rows, length = activity.shape
    edge = 2 * lines
    shape = jax.ShapeDtypeStruct((edge + 8, length), F32)
    out = pl.BlockSpec((edge + 8, length), lambda i: (0, 0))
    return pl.pallas_call(
        halo_kernel,
        out_shape=(shape, shape),
        grid=(1,),
        in_specs=[
            SPEC_SMEM,
            pl.BlockSpec((edge, length), lambda i: (0, 0)),
            pl.BlockSpec((edge, length), lambda i: (rows // edge - 1, 0)),
        ],
        out_specs=(out, out),
        compiler_params=params(8),
        cost_estimate=cost(0, MIB),
        name="halo",
    )(width, activity, activity)


def blur(lines, width, activity, low, high, blurred):
    planes = activity.shape[0] // lines

    def put(at, w, here, down, up):
        value = (1.0 - 2.0 * w) * here + w * (down + up)
        blurred[pl.ds(at, lines), :] = value.astype(BF16)

    def plane(z):
        return activity[z * lines : (z + 1) * lines, :]

    near_low, near_high = low[lines : 2 * lines, :], high[0:lines, :]
    wide_low = low[2 * lines : 2 * lines + 1, :]
    wide_high = high[2 * lines : 2 * lines + 1, :]
    put(0, wide_low, near_low, low[0:lines, :], plane(0))
    put(lines, width[0], plane(0), near_low, plane(1))
    put(planes * lines, width[planes - 1], plane(planes - 1), plane(planes - 2), near_high)
    put((planes + 1) * lines, wide_high, near_high, plane(planes - 1), high[lines : 2 * lines, :])

    def inner(z, carry):
        start = pl.multiple_of(z * lines, lines)
        here = activity[pl.ds(start, lines), :]
        down = activity[pl.ds(pl.multiple_of(start - lines, lines), lines), :]
        up = activity[pl.ds(pl.multiple_of(start + lines, lines), lines), :]
        put(pl.multiple_of(start + lines, lines), width[z], here, down, up)
        return carry

    lax.fori_loop(1, planes - 1, inner, 0)


def front_kernel(lines, *refs):
    if lines is not None:
        spacing, offset, width, activity, low, high, blurred, k_out, r_out = refs
        blur(lines, width, activity, low, high, blurred)
    else:
        spacing, offset, blurred, k_out, r_out = refs
    extended, length = blurred.shape
    angles = spacing.shape[0]
    bins = k_out.shape[0] // angles
    step_width = length / bins
    deviation = 0.25 * step_width
    scale = 1.0 / (deviation * math.sqrt(2.0 * math.pi))
    sharp = -math.log2(math.e) / (2.0 * deviation * deviation)
    some = 32
    pair = 2
    voxel = iota((1, length), 1).astype(F32) + 0.5 - length / 2
    bin_at = iota((some, 1), 0).astype(F32) + 0.5 - bins / 2

    def group(q, carry):
        begin = pl.multiple_of(q * pair * bins, pair * bins)
        for i in range(pair * bins // some):
            a = q * pair + i * some // bins
            centre = (bin_at + float(i * some % bins)) * spacing[a] + offset[a]
            distance = voxel - centre
            value = jnp.exp2(distance * distance * sharp) * scale
            k_out[pl.ds(begin + i * some, some), :] = value.astype(BF16)
        columns = pl.ds(begin, pair * bins)
        estimate = matmul(blurred[...], k_out[columns, :], (1, 1))
        r_out[:, columns] = 1.0 / (estimate + BACKGROUND)
        return carry

    lax.fori_loop(0, angles // pair, group, 0)


def front(spacing, offset, blurred, bins, planes_in=None):
    (angles,) = spacing.shape
    wide = angles * bins
    lines = None
    if planes_in is None:
        extended, length = blurred.shape
        operands, specs = [blurred], [SPEC_VMEM]
    else:
        *operands, lines = planes_in
        rows, length = operands[1].shape
        extended = rows + 2 * lines
        specs = [SPEC_SMEM] + [SPEC_VMEM] * 3
    shapes = [
        jax.ShapeDtypeStruct((wide, length), BF16),
        jax.ShapeDtypeStruct((extended, wide), F32),
    ]
    if planes_in is not None:
        shapes.insert(0, jax.ShapeDtypeStruct((extended, length), BF16))
    return pl.pallas_call(
        functools.partial(front_kernel, lines),
        out_shape=shapes,
        in_specs=[SPEC_SMEM, SPEC_SMEM] + specs,
        out_specs=[SPEC_VMEM] * len(shapes),
        compiler_params=params(LIMIT_FRONT),
        cost_estimate=cost(2 * extended * length * wide, 12 * MIB),
        name="front",
    )(spacing, offset, *operands)


def back_kernel(counts, has_prior, last, lines, *refs):
    refs = list(refs)

    def take(number):
        taken = refs[:number]
        del refs[:number]
        return taken

    received = take(len(counts))
    k_buf, r_buf = take(2)
    (prior,) = take(1) if has_prior else (None,)
    if last:
        width, low, high, activity, sensitivity = take(5)
    (out,) = take(1)
    (rounded,) = take(1)
    if last:
        total, updated, sems = take(3)
    sources = [(ref, s) for ref, count in zip(received, counts) for s in range(count)]
    bins = received[0].shape[-1]
    extended, wide = r_buf.shape
    length = k_buf.shape[1]
    angles = wide // bins
    planes = extended // lines - 2
    body = planes * PAIR
    group = bins // PAIR

    rows = [
        ref[s, body + 2 * PAIR : body + 2 * PAIR + META, :].astype(F32)[0:8, :] for ref, s in sources
    ]
    lane = iota((8, bins), 1)
    named = []
    for kind in range(3):
        parts = []
        for first in range(0, len(rows), group):
            codes = jnp.zeros((8, bins), F32)
            for i in range(first, min(first + group, len(rows))):
                own = jnp.where(lane // PAIR == kind, rows[i], 0.0)
                codes = codes + pltpu.roll(own, (i - first - kind) % group * PAIR, 1)
            parts.append(codes[0:1, :])
        codes = jnp.concatenate(parts, axis=1).astype(I32)
        named.append(one_hot(codes - 1 == iota((angles * lines, codes.shape[1]), 0)))

    def sums(kind, at, start):
        held = [ref[s, pl.ds(at, PAIR), :] for ref, s in sources]
        spare = -len(held) % group * PAIR
        if spare:
            held.append(jnp.zeros((spare, bins), BF16))
        sums = matmul(named[kind], jnp.concatenate(held))
        for a in range(angles):
            place = (pl.ds(start, lines), pl.ds(a * bins, bins))
            rounded[place] = (sums[a * lines : (a + 1) * lines, :] * r_buf[place]).astype(BF16)

    sums(1, body, 0)
    sums(2, body + PAIR, extended - lines)

    def inner(z, carry):
        sums(0, pl.multiple_of(z * PAIR, PAIR), pl.multiple_of((z + 1) * lines, lines))
        return carry

    lax.fori_loop(0, planes, inner, 0, unroll=4)

    block = 256
    steps = length // block

    def project(columns):
        value = matmul(rounded[...], k_buf[:, columns])
        return prior[:, columns] + value if has_prior else value

    if not last:

        def step(i, carry):
            columns = pl.ds(pl.multiple_of(i * block, block), block)
            out[:, columns] = project(columns)
            return carry

        lax.fori_loop(0, steps, step, 0)
        return

    def write(i):
        columns = pl.ds(i * block, block)
        return pltpu.make_async_copy(updated.at[i % 2], out.at[:, columns], sems.at[i % 2])

    for i in range(steps):
        columns = pl.ds(i * block, block)
        total[...] = project(columns)
        if i >= 2:
            write(i - 2).wait()

        def smooth(z, w_down, w_up, i=i, columns=columns):
            start = z * lines
            w = width[z]
            down = total[pl.ds(start, lines), :]
            here = total[pl.ds(start + lines, lines), :]
            up = total[pl.ds(start + 2 * lines, lines), :]
            smoothed = (1.0 - 2.0 * w) * here + w_down * down + w_up * up
            at = pl.ds(start, lines)
            value = activity[at, columns] * smoothed / sensitivity[at, columns]
            updated[i % 2, at, :] = value

        def inside(z, carry, smooth=smooth):
            smooth(z, width[z - 1], width[z + 1])
            return carry

        smooth(0, low[2 * lines : 2 * lines + 1, 0:block], width[1])
        lax.fori_loop(1, planes - 1, inside, 0, unroll=10)
        smooth(planes - 1, width[planes - 2], high[2 * lines : 2 * lines + 1, 0:block])
        write(i).start()
    for i in range(max(0, steps - 2), steps):
        write(i).wait()


def back(pieces, k, r, prior, final, lines):
    extended, wide = r.shape
    _, length = k.shape
    operands = [*pieces, k, r]
    specs = [SPEC_VMEM] * len(operands)
    if prior is not None:
        operands.append(prior)
        specs.append(SPEC_VMEM)
    scratch = [VMEM((extended, wide), BF16)]
    shape = (extended, length)
    if final is not None:
        rows = extended - 2 * lines
        operands += final
        specs += [SPEC_SMEM] + [SPEC_VMEM] * 4
        scratch += [
            VMEM((extended, 256), F32),
            VMEM((2, rows, 256), F32),
            pltpu.SemaphoreType.DMA((2,)),
        ]
        shape = (rows, length)
    return pl.pallas_call(
        functools.partial(
            back_kernel,
            [piece.shape[0] for piece in pieces],
            prior is not None,
            final is not None,
            lines,
        ),
        out_shape=jax.ShapeDtypeStruct(shape, F32),
        in_specs=specs,
        out_specs=SPEC_VMEM if final is None else SPEC_HBM,
        scratch_shapes=scratch,
        compiler_params=params(LIMIT_BACK if final is None else LIMIT_UPDATE),
        cost_estimate=cost(2 * extended * length * wide, 12 * MIB),
        name="back" if final is None else "update",
    )(*operands)


def swap(value):
    return lax.ppermute(value, "view", [(0, 1), (1, 0)])


def flip(value, mask):
    size = lax.axis_size("slab")
    return lax.ppermute(value, "slab", [(i, i ^ mask) for i in range(size)])


def on_device(
    activity, sensitivity, psf_width, measured, block_slab, block_line, block_angle, subset_views
):
    planes, lines, length = activity.shape
    _, blocks, _, bins = measured.shape
    slabs, view_count = lax.axis_size("slab"), lax.axis_size("view")
    assert 2 * blocks <= SLOTS * slabs and 2 * blocks == bins and slabs <= WIDE
    assert subset_views.shape[1] * lines <= 256

    flat = activity.reshape(planes * lines, length)
    raw = measured.reshape(blocks * planes, bins)
    parts = [block_slab.reshape(1, blocks), block_line, block_angle]
    parts = [jnp.pad(part, ((i, 7 - i), (0, bins - blocks))) for i, part in enumerate(parts)]
    table = functools.reduce(jnp.add, parts)
    raws, tables = [raw, flip(raw, 1)], [table, flip(table, 1)]
    ups = [(i, i + 1) for i in range(slabs - 1)]
    downs = [(j, i) for i, j in ups]
    low_mine, high_mine = halo(psf_width, flat, lines)
    low = lax.ppermute(low_mine, "slab", ups)
    high = lax.ppermute(high_mine, "slab", downs)
    chips = slabs // 2
    if slabs == 16 and view_count == 2:
        send = bucket(raws, tables, chips, True, planes, lines)
        far = [flip(send[j : j + 1], 2 * j) for j in range(4, 8)]
        near = [send[0:1]] + [flip(send[j : j + 1], 2 * j) for j in range(1, 4)]
        over = [swap(jnp.concatenate(part)) for part in (near, far[:2], far[2:])]
        pieces = [near + far, over]
        views = [subset_views[0], swap(subset_views[0])]
    else:
        send = bucket(raws, tables, chips, False, planes, lines)
        cores = [[2 * chip + core for chip in range(chips)] for core in range(2)]
        own = lax.all_to_all(
            send, "slab", split_axis=0, concat_axis=0, axis_index_groups=cores, tiled=True
        )
        everyone = lax.all_gather(own, "view")
        pieces = [[everyone[g]] for g in range(view_count)]
        gathered = lax.all_gather(subset_views[0], "view")
        views = [gathered[g] for g in range(view_count)]

    step_width = length / bins
    fronts = []
    for view in views:
        angle = math.pi * view.astype(F32) / VIEWS_ALL
        spacing = step_width * (0.75 + 0.25 * jnp.cos(2.0 * angle))
        offset = 1.5 * step_width * jnp.sin(angle)
        if not fronts:
            planes_in = (psf_width, flat, low, high, lines)
            blurred, *made = front(spacing, offset, None, bins, planes_in)
        else:
            made = front(spacing, offset, blurred, bins)
        fronts.append(made)

    result = None
    for g in range(view_count):
        final = None
        if g == view_count - 1:
            final = [psf_width, low, high, flat, sensitivity.reshape(planes * lines, length)]
        result = back(pieces[g], *fronts[g], result, final, lines)
    return result.reshape(planes, lines, length)


def solution(mesh):
    in_specs = (
        P("slab", None, None),
        P("slab", None, None),
        P("slab"),
        P("view", "slab", None, None),
        P("view", "slab", None),
        P("view", "slab"),
        P("view", "slab"),
        P("view", None),
    )
    out_specs = P("slab", None, None)
    return jax.shard_map(
        on_device, mesh=mesh, in_specs=in_specs, out_specs=out_specs, check_vma=False
    )
```

```python
import functools
import math

import jax
import jax.numpy as jnp
from jax import lax
from jax.experimental import pallas as pl
from jax.experimental.pallas import tpu as pltpu
from jax.sharding import PartitionSpec as P

VIEWS_ALL = 336
BACKGROUND = 0.05
SLOTS = 8
PAIR = 2 * SLOTS
META = 16
WIDE = 64
F32 = jnp.float32
BF16 = jnp.bfloat16
I32 = jnp.int32
SMEM = pltpu.SMEM
VMEM = pltpu.VMEM
MIB = 1024 * 1024
BLOCK = 512
LIMIT_FRONT = 12
LIMIT_BACK = 14
LIMIT_UPDATE = 20


def iota(shape, dim):
    return lax.broadcasted_iota(I32, shape, dim)


def matmul(a, b, contract=(1, 0)):
    dims = (((contract[0],), (contract[1],)), ((), ()))
    return lax.dot_general(a, b, dims, preferred_element_type=F32)


def params(limit):
    return pltpu.CompilerParams(vmem_limit_bytes=limit * MIB)


def cost(flops, moved):
    return pl.CostEstimate(flops=flops, bytes_accessed=moved, transcendentals=0)


SPEC_SMEM = pl.BlockSpec(memory_space=SMEM)
SPEC_VMEM = pl.BlockSpec(memory_space=VMEM)
SPEC_ANY = pl.BlockSpec(memory_space=pl.ANY)
SPEC_HBM = pl.BlockSpec(memory_space=pltpu.HBM)


def one_hot(mask):
    return mask.astype(F32).astype(BF16)


def bucket_kernel(chips, relative, planes, lines, *refs):
    raws, tables = refs[0:2], refs[2:4]
    out, wide, flat = refs[4:]
    rows, bins = raws[0].shape
    blocks = rows // planes
    both = 2 * blocks
    me = lax.axis_index("slab")

    for i, raw in enumerate(raws):
        wide[i] = raw[...].astype(F32)

    def turn(z, carry):
        column = pl.ds(pl.multiple_of(z * bins, bins), bins)
        for i in range(2):
            part = wide[i, pl.ds(z, blocks, stride=planes), :]
            flat[i * blocks : (i + 1) * blocks, column] = part.astype(BF16)
        return carry

    lax.fori_loop(0, planes, turn, 0, unroll=4)

    def lanes(row):
        return tables[0][row : row + 1, :] + pltpu.roll(tables[1][row : row + 1, :], blocks, 1)

    slab, code = lanes(0), (lanes(2) * lines + lanes(1) + 1).astype(F32)
    shape = (both, both)
    earlier = (iota(shape, 0) < iota(shape, 1)) & (iota(shape, 0) // blocks == iota(shape, 1) // blocks)
    names = (iota((WIDE, both), 0) == slab).astype(F32)
    ranks = matmul(names.astype(BF16), one_hot(earlier))
    slot = jnp.sum(names * ranks, axis=0, keepdims=True).astype(I32)
    slot = slot + iota((1, both), 1) // blocks * SLOTS

    def target(chip):
        return (2 * chip) ^ me if relative else 2 * chip + (me & 1)

    row = iota((chips * PAIR, both), 0)
    aim = target(row // PAIR)
    here = slot == row % PAIR
    chosen = one_hot((slab == aim) & here)

    some = 2

    def deal(i, carry):
        column = pl.ds(pl.multiple_of(i * some * bins, some * bins), some * bins)
        dealt = matmul(chosen, flat[:, column]).astype(BF16)
        for j in range(some):
            at = pl.ds(pl.multiple_of((i * some + j) * PAIR, PAIR), PAIR)
            for chip in range(chips):
                part = dealt[chip * PAIR : (chip + 1) * PAIR, j * bins : (j + 1) * bins]
                out[chip, at, :] = part
        return carry

    lax.fori_loop(0, planes // some, deal, 0, unroll=4)

    body = planes * PAIR
    aim_row = target(iota((chips, both), 0))
    lane = iota((bins, both), 0)
    codes = jnp.zeros((chips, bins), F32)
    for kind, (shift, z) in enumerate(((0, None), (-1, planes - 1), (1, 0))):
        picked = ((slab == aim_row + shift).astype(F32) * code).astype(BF16)
        codes = codes + matmul(picked, one_hot(slot + kind * PAIR == lane), (1, 1))
        if kind:
            edge = one_hot((slab == aim + shift) & here)
            dealt = matmul(edge, flat[:, z * bins : (z + 1) * bins]).astype(BF16)
            at = body + (kind - 1) * PAIR
            for chip in range(chips):
                out[chip, at : at + PAIR, :] = dealt[chip * PAIR : (chip + 1) * PAIR, :]
    codes = codes.astype(BF16)
    for chip in range(chips):
        spread = jnp.broadcast_to(codes[chip : chip + 1, :].astype(F32), (META, bins))
        out[chip, body + 2 * PAIR :, :] = spread.astype(BF16)


def bucket(raws, tables, chips, relative, planes, lines):
    rows, bins = raws[0].shape
    sent = (planes + 2) * PAIR + META
    return pl.pallas_call(
        functools.partial(bucket_kernel, chips, relative, planes, lines),
        out_shape=jax.ShapeDtypeStruct((chips, sent, bins), BF16),
        in_specs=[SPEC_VMEM] * 4,
        out_specs=SPEC_VMEM,
        scratch_shapes=[VMEM((2, rows, bins), F32), VMEM((2 * rows // planes, planes * bins), BF16)],
        compiler_params=params(24),
        cost_estimate=cost(10**8, 4 * MIB),
        name="bucket",
    )(*raws, *tables)


def relay_kernel(count, unread, *refs):
    arrived, out = refs[:count], refs[count + unread]
    for i, ref in enumerate(arrived):
        out[i] = ref[0]


def relay(arrived, passed, after):
    count = len(arrived)
    like = [jax.ShapeDtypeStruct(value.shape, value.dtype) for value in passed]
    joined, *rest = pl.pallas_call(
        functools.partial(relay_kernel, count, len(passed) + len(after)),
        out_shape=[jax.ShapeDtypeStruct((count, *arrived[0].shape[1:]), BF16), *like],
        in_specs=[SPEC_VMEM] * count + [SPEC_ANY] * (len(passed) + len(after)),
        out_specs=[SPEC_VMEM] + [SPEC_ANY] * len(passed),
        input_output_aliases={count + i: 1 + i for i in range(len(passed))},
        compiler_params=params(8),
        cost_estimate=cost(0, MIB),
        name="relay",
    )(*arrived, *passed, *after)
    return joined, rest


def behind_kernel(*refs):
    del refs


def behind(passed, after):
    return pl.pallas_call(
        behind_kernel,
        out_shape=[jax.ShapeDtypeStruct(value.shape, value.dtype) for value in passed],
        in_specs=[SPEC_ANY] * (len(passed) + 1),
        out_specs=[SPEC_ANY] * len(passed),
        input_output_aliases={i: i for i in range(len(passed))},
        compiler_params=params(8),
        cost_estimate=cost(0, 0),
        name="behind",
    )(*passed, after)


def mix(w, here, down, up):
    return ((1.0 - 2.0 * w) * here + w * (down + up)).astype(BF16)


def blur_kernel(lines, width, activity, _, blurred, low_out, high_out):
    rows, length = activity.shape
    planes = rows // lines
    edge = 2 * lines
    low_out[0:edge, :] = activity[rows - edge :, :]
    low_out[edge : edge + 8, :] = jnp.full((8, length), width[planes - 1], F32)
    high_out[0:edge, :] = activity[0:edge, :]
    high_out[edge : edge + 8, :] = jnp.full((8, length), width[0], F32)

    def inner(z, carry):
        start = pl.multiple_of(z * lines, lines)
        here = activity[pl.ds(start, lines), :]
        down = activity[pl.ds(pl.multiple_of(start - lines, lines), lines), :]
        up = activity[pl.ds(pl.multiple_of(start + lines, lines), lines), :]
        at = pl.ds(pl.multiple_of(start - lines, lines), lines)
        blurred[at, :] = mix(width[z], here, down, up)
        return carry

    lax.fori_loop(1, planes - 1, inner, 0)


def blur(width, activity, after, lines):
    rows, length = activity.shape
    shape = jax.ShapeDtypeStruct((2 * lines + 8, length), F32)
    return pl.pallas_call(
        functools.partial(blur_kernel, lines),
        out_shape=(jax.ShapeDtypeStruct((rows - 2 * lines, length), BF16), shape, shape),
        in_specs=[SPEC_SMEM, SPEC_VMEM, SPEC_ANY],
        out_specs=(SPEC_VMEM, SPEC_VMEM, SPEC_VMEM),
        compiler_params=params(12),
        cost_estimate=cost(0, 4 * MIB),
        name="blur",
    )(width, activity, after)


def edge_kernel(lines, groups, after, width, low, high, activity, sensitivity, *refs):
    kernels, refs = refs[:groups], refs[groups + after :]
    edges, gain, blurred = refs[:groups], refs[groups], refs[groups + 1]
    rows, length = activity.shape
    planes = rows // lines
    bins = 256

    def plane(z):
        return activity[z * lines : (z + 1) * lines, :]

    near_low, near_high = low[lines : 2 * lines, :], high[0:lines, :]
    wide_low = low[2 * lines : 2 * lines + 1, :]
    wide_high = high[2 * lines : 2 * lines + 1, :]
    final, before = plane(planes - 1), plane(planes - 2)
    blurred[0:lines, :] = mix(wide_low, near_low, low[0:lines, :], plane(0))
    blurred[lines : 2 * lines, :] = mix(width[0], plane(0), near_low, plane(1))
    blurred[2 * lines : 3 * lines, :] = mix(width[planes - 1], final, before, near_high)
    blurred[3 * lines : 4 * lines, :] = mix(wide_high, near_high, final, high[lines : 2 * lines, :])
    for kernel, edge in zip(kernels, edges):

        def project(i, carry, kernel=kernel, edge=edge):
            columns = pl.ds(pl.multiple_of(i * bins, bins), bins)
            estimate = matmul(blurred[...], kernel[columns, :], (1, 1))
            edge[:, columns] = 1.0 / (estimate + BACKGROUND)
            return carry

        lax.fori_loop(0, kernel.shape[0] // bins, project, 0)

    def divide(i, carry):
        at = pl.ds(pl.multiple_of(i * lines, lines), lines)
        gain[at, :] = activity[at, :] / sensitivity[at, :]
        return carry

    lax.fori_loop(0, planes, divide, 0)


def edge(width, low, high, activity, sensitivity, kernels, after, lines):
    rows, length = activity.shape
    groups = len(kernels)
    shape = jax.ShapeDtypeStruct((4 * lines, kernels[0].shape[0]), F32)
    *edges, gain = pl.pallas_call(
        functools.partial(edge_kernel, lines, groups, len(after)),
        out_shape=[shape] * groups + [jax.ShapeDtypeStruct((rows, length), F32)],
        in_specs=[SPEC_SMEM] + [SPEC_VMEM] * (4 + groups) + [SPEC_ANY] * len(after),
        out_specs=[SPEC_VMEM] * (groups + 1),
        scratch_shapes=[VMEM((4 * lines, length), BF16)],
        compiler_params=params(LIMIT_BACK),
        cost_estimate=cost(groups * 2 * 4 * lines * length * 1024, 12 * MIB),
        name="edge",
    )(width, low, high, activity, sensitivity, *kernels, *after)
    return edges, gain


def front_kernel(after, spacing, offset, blurred, *refs):
    k_out, r_out = refs[after:]
    length = blurred.shape[1]
    angles = spacing.shape[0]
    bins = k_out.shape[0] // angles
    step_width = length / bins
    deviation = 0.25 * step_width
    scale = 1.0 / (deviation * math.sqrt(2.0 * math.pi))
    sharp = -math.log2(math.e) / (2.0 * deviation * deviation)
    some = 32
    pair = 4
    voxel = iota((1, length), 1).astype(F32) + 0.5 - length / 2
    bin_at = iota((some, 1), 0).astype(F32) + 0.5 - bins / 2

    def group(q, carry):
        begin = pl.multiple_of(q * pair * bins, pair * bins)
        for i in range(pair * bins // some):
            a = q * pair + i * some // bins
            centre = (bin_at + float(i * some % bins)) * spacing[a] + offset[a]
            distance = voxel - centre
            value = jnp.exp2(distance * distance * sharp) * scale
            k_out[pl.ds(begin + i * some, some), :] = value.astype(BF16)
        columns = pl.ds(begin, pair * bins)
        estimate = matmul(blurred[...], k_out[columns, :], (1, 1))
        r_out[:, columns] = 1.0 / (estimate + BACKGROUND)
        return carry

    lax.fori_loop(0, angles // pair, group, 0)


def front(spacing, offset, blurred, bins, after=()):
    (angles,) = spacing.shape
    wide = angles * bins
    rows, length = blurred.shape
    return pl.pallas_call(
        functools.partial(front_kernel, len(after)),
        out_shape=(
            jax.ShapeDtypeStruct((wide, length), BF16),
            jax.ShapeDtypeStruct((rows, wide), F32),
        ),
        in_specs=[SPEC_SMEM, SPEC_SMEM, SPEC_VMEM] + [SPEC_ANY] * len(after),
        out_specs=(SPEC_VMEM, SPEC_VMEM),
        compiler_params=params(LIMIT_FRONT),
        cost_estimate=cost(2 * rows * length * wide, 8 * MIB),
        name="front",
    )(spacing, offset, blurred, *after)


def back_kernel(counts, has_prior, last, lines, *refs):
    refs = list(refs)

    def take(number):
        taken = refs[:number]
        del refs[:number]
        return taken

    received = take(len(counts))
    k_buf, r_buf, edge_buf = take(3)
    (prior,) = take(1) if has_prior else (None,)
    if last:
        width, low, high, gain = take(4)
    (out,) = take(1)
    (rounded,) = take(1)
    if last:
        total, updated, sems = take(3)
    sources = [(ref, s) for ref, count in zip(received, counts) for s in range(count)]
    bins = received[0].shape[-1]
    extended, wide = rounded.shape
    length = k_buf.shape[1]
    angles = wide // bins
    planes = extended // lines - 2
    body = planes * PAIR
    group = bins // PAIR

    rows = [
        ref[s, body + 2 * PAIR : body + 2 * PAIR + META, :].astype(F32)[0:8, :] for ref, s in sources
    ]
    lane = iota((8, bins), 1)
    named = []
    for kind in range(3):
        parts = []
        for first in range(0, len(rows), group):
            codes = jnp.zeros((8, bins), F32)
            for i in range(first, min(first + group, len(rows))):
                own = jnp.where(lane // PAIR == kind, rows[i], 0.0)
                codes = codes + pltpu.roll(own, (i - first - kind) % group * PAIR, 1)
            parts.append(codes[0:1, :])
        codes = jnp.concatenate(parts, axis=1).astype(I32)
        named.append(one_hot(codes - 1 == iota((angles * lines, codes.shape[1]), 0)))

    def sums(kind, at, start, inverse, first):
        held = [ref[s, pl.ds(at, PAIR), :] for ref, s in sources]
        spare = -len(held) % group * PAIR
        if spare:
            held.append(jnp.zeros((spare, bins), BF16))
        sums = matmul(named[kind], jnp.concatenate(held))
        for a in range(angles):
            columns = pl.ds(a * bins, bins)
            ratio = sums[a * lines : (a + 1) * lines, :] * inverse[pl.ds(first, lines), columns]
            rounded[pl.ds(start, lines), columns] = ratio.astype(BF16)

    sums(1, body, 0, edge_buf, 0)
    sums(0, 0, lines, edge_buf, lines)
    sums(0, body - PAIR, extended - 2 * lines, edge_buf, 2 * lines)
    sums(2, body + PAIR, extended - lines, edge_buf, 3 * lines)

    def inner(z, carry):
        start = pl.multiple_of(z * lines, lines)
        first = pl.multiple_of(start - lines, lines)
        sums(0, pl.multiple_of(z * PAIR, PAIR), start + lines, r_buf, first)
        return carry

    lax.fori_loop(1, planes - 1, inner, 0, unroll=5)

    block = total.shape[2] if last else 512
    steps = length // block

    def project(columns):
        value = matmul(rounded[...], k_buf[:, columns])
        return prior[:, columns] + value if has_prior else value

    if not last:

        def step(i, carry):
            columns = pl.ds(pl.multiple_of(i * block, block), block)
            out[:, columns] = project(columns)
            return carry

        lax.fori_loop(0, steps, step, 0)
        return

    def write(i):
        columns = pl.ds(i * block, block)
        return pltpu.make_async_copy(updated.at[i % 2], out.at[:, columns], sems.at[i % 2])

    def smooth(i):
        held, columns = total.at[i % 2], pl.ds(i * block, block)
        for z in range(planes):
            edge_low = low[2 * lines : 2 * lines + 1, 0:block] if z == 0 else width[z - 1]
            edge_high = high[2 * lines : 2 * lines + 1, 0:block] if z == planes - 1 else width[z + 1]
            start = z * lines
            down = held[start : start + lines, :]
            here = held[start + lines : start + 2 * lines, :]
            up = held[start + 2 * lines : start + 3 * lines, :]
            value = (1.0 - 2.0 * width[z]) * here + edge_low * down + edge_high * up
            at = pl.ds(start, lines)
            updated[i % 2, at, :] = value * gain[at, columns]

    for i in range(steps + 1):
        if i >= 3:
            write(i - 3).wait()
        if i < steps:
            total[i % 2] = project(pl.ds(i * block, block))
        if i:
            smooth(i - 1)
            write(i - 1).start()
    for i in range(max(0, steps - 2), steps):
        write(i).wait()


def back(pieces, k, r, edges, prior, final, lines):
    rows, wide = r.shape
    extended = rows + 4 * lines
    _, length = k.shape
    operands = [*pieces, k, r, edges]
    specs = [SPEC_VMEM] * len(operands)
    if prior is not None:
        operands.append(prior)
        specs.append(SPEC_VMEM)
    scratch = [VMEM((extended, wide), BF16)]
    shape = (extended, length)
    if final is not None:
        rows = extended - 2 * lines
        operands += final
        specs += [SPEC_SMEM] + [SPEC_VMEM] * 3
        scratch += [
            VMEM((2, extended, BLOCK), F32),
            VMEM((2, rows, BLOCK), F32),
            pltpu.SemaphoreType.DMA((2,)),
        ]
        shape = (rows, length)
    return pl.pallas_call(
        functools.partial(
            back_kernel,
            [piece.shape[0] for piece in pieces],
            prior is not None,
            final is not None,
            lines,
        ),
        out_shape=jax.ShapeDtypeStruct(shape, F32),
        in_specs=specs,
        out_specs=SPEC_VMEM if final is None else SPEC_HBM,
        scratch_shapes=scratch,
        compiler_params=params(LIMIT_BACK if final is None else LIMIT_UPDATE),
        cost_estimate=cost(2 * extended * length * wide, 12 * MIB),
        name="back" if final is None else "update",
    )(*operands)


def swap(value):
    return lax.ppermute(value, "view", [(0, 1), (1, 0)])


def flip(value, mask):
    size = lax.axis_size("slab")
    return lax.ppermute(value, "slab", [(i, i ^ mask) for i in range(size)])


def on_device(
    activity, sensitivity, psf_width, measured, block_slab, block_line, block_angle, subset_views
):
    planes, lines, length = activity.shape
    _, blocks, _, bins = measured.shape
    slabs, view_count = lax.axis_size("slab"), lax.axis_size("view")
    assert 2 * blocks <= SLOTS * slabs and 2 * blocks == bins and slabs <= WIDE
    assert subset_views.shape[1] * lines <= 256

    flat = activity.reshape(planes * lines, length)
    raw = measured.reshape(blocks * planes, bins)
    parts = [block_slab.reshape(1, blocks), block_line, block_angle]
    parts = [jnp.pad(part, ((i, 7 - i), (0, bins - blocks))) for i, part in enumerate(parts)]
    table = functools.reduce(jnp.add, parts)
    raws, tables = [raw, flip(raw, 1)], [table, flip(table, 1)]
    ups = [(i, i + 1) for i in range(slabs - 1)]
    downs = [(j, i) for i, j in ups]
    chips = slabs // 2
    step_width = length / bins

    def forward(view, blurred, behind=()):
        angle = math.pi * view.astype(F32) / VIEWS_ALL
        spacing = step_width * (0.75 + 0.25 * jnp.cos(2.0 * angle))
        offset = 1.5 * step_width * jnp.sin(angle)
        return front(spacing, offset, blurred, bins, behind)

    if slabs == 16 and view_count == 2:
        other = swap(subset_views[0])
        send = bucket(raws, tables, chips, True, planes, lines)
        blurred, *mine = blur(psf_width, flat, send, lines)
        near = [send[0:1]] + [flip(send[j : j + 1], 2 * j) for j in range(1, 4)]
        far = [flip(send[j : j + 1], 2 * j) for j in (4, 5)]
        fronts = [forward(subset_views[0], blurred)]
        joined, passed = relay(near, [send[6:7], send[7:8], *mine], [fronts[0][0]])
        far += [flip(passed[0], 12), flip(passed[1], 14)]
        mine = passed[2:]
        over = [swap(joined)] + [swap(jnp.concatenate(part)) for part in (far[:2], far[2:])]
        pieces = [[joined, *far], over]
        fronts.append(forward(other, blurred, [joined]))
        behind_edge = [over[0]]
    else:
        send = bucket(raws, tables, chips, False, planes, lines)
        blurred, *mine = blur(psf_width, flat, send, lines)
        cores = [[2 * chip + core for chip in range(chips)] for core in range(2)]
        own = lax.all_to_all(
            send, "slab", split_axis=0, concat_axis=0, axis_index_groups=cores, tiled=True
        )
        everyone = lax.all_gather(own, "view")
        pieces = [[everyone[g]] for g in range(view_count)]
        gathered = lax.all_gather(subset_views[0], "view")
        fronts = [forward(gathered[g], blurred) for g in range(view_count)]
        behind_edge = []

    low = lax.ppermute(mine[0], "slab", ups)
    high = lax.ppermute(mine[1], "slab", downs)
    kernels, inverses = zip(*fronts)
    whole = sensitivity.reshape(planes * lines, length)
    edges, gain = edge(psf_width, low, high, flat, whole, kernels, behind_edge, lines)

    result = None
    for g in range(view_count):
        final = None
        if g == view_count - 1:
            final = [psf_width, low, high, gain]
        result = back(pieces[g], kernels[g], inverses[g], edges[g], result, final, lines)
    return result.reshape(planes, lines, length)


def solution(mesh):
    in_specs = (
        P("slab", None, None),
        P("slab", None, None),
        P("slab"),
        P("view", "slab", None, None),
        P("view", "slab", None),
        P("view", "slab"),
        P("view", "slab"),
        P("view", None),
    )
    out_specs = P("slab", None, None)
    return jax.shard_map(
        on_device, mesh=mesh, in_specs=in_specs, out_specs=out_specs, check_vma=False
    )
```

```python
import functools
import math

import jax
import jax.numpy as jnp
from jax import lax
from jax.experimental import pallas as pl
from jax.experimental.pallas import tpu as pltpu
from jax.sharding import PartitionSpec as P

VIEWS_ALL = 336
BACKGROUND = 0.05
SLOTS = 8
PAIR = 2 * SLOTS
META = 16
WIDE = 64
F32 = jnp.float32
BF16 = jnp.bfloat16
I32 = jnp.int32
SMEM = pltpu.SMEM
VMEM = pltpu.VMEM
MIB = 1024 * 1024
BLOCK = 512
LIMIT_FRONT = 12
LIMIT_BACK = 14
LIMIT_UPDATE = 20


def iota(shape, dim):
    return lax.broadcasted_iota(I32, shape, dim)


def matmul(a, b, contract=(1, 0)):
    dims = (((contract[0],), (contract[1],)), ((), ()))
    return lax.dot_general(a, b, dims, preferred_element_type=F32)


def params(limit):
    return pltpu.CompilerParams(vmem_limit_bytes=limit * MIB)


def cost(flops, moved):
    del flops, moved
    return pl.CostEstimate(flops=0, bytes_accessed=0, transcendentals=0)


SPEC_SMEM = pl.BlockSpec(memory_space=SMEM)
SPEC_VMEM = pl.BlockSpec(memory_space=VMEM)
SPEC_ANY = pl.BlockSpec(memory_space=pl.ANY)
SPEC_HBM = pl.BlockSpec(memory_space=pltpu.HBM)


def one_hot(mask):
    return mask.astype(F32).astype(BF16)


def bucket_kernel(chips, relative, planes, lines, *refs):
    raws, tables = refs[0:2], refs[2:4]
    out, wide, flat = refs[4:]
    rows, bins = raws[0].shape
    blocks = rows // planes
    both = 2 * blocks
    me = lax.axis_index("slab")

    for i, raw in enumerate(raws):
        wide[i] = raw[...].astype(F32)

    def turn(z, carry):
        column = pl.ds(pl.multiple_of(z * bins, bins), bins)
        for i in range(2):
            part = wide[i, pl.ds(z, blocks, stride=planes), :]
            flat[i * blocks : (i + 1) * blocks, column] = part.astype(BF16)
        return carry

    lax.fori_loop(0, planes, turn, 0, unroll=4)

    def lanes(row):
        return tables[0][row : row + 1, :] + pltpu.roll(tables[1][row : row + 1, :], blocks, 1)

    slab, code = lanes(0), (lanes(2) * lines + lanes(1) + 1).astype(F32)
    shape = (both, both)
    earlier = (iota(shape, 0) < iota(shape, 1)) & (iota(shape, 0) // blocks == iota(shape, 1) // blocks)
    names = (iota((WIDE, both), 0) == slab).astype(F32)
    ranks = matmul(names.astype(BF16), one_hot(earlier))
    slot = jnp.sum(names * ranks, axis=0, keepdims=True).astype(I32)
    slot = slot + iota((1, both), 1) // blocks * SLOTS

    def target(chip):
        return (2 * chip) ^ me if relative else 2 * chip + (me & 1)

    row = iota((chips * PAIR, both), 0)
    aim = target(row // PAIR)
    here = slot == row % PAIR
    chosen = one_hot((slab == aim) & here)

    some = 2

    def deal(i, carry):
        column = pl.ds(pl.multiple_of(i * some * bins, some * bins), some * bins)
        dealt = matmul(chosen, flat[:, column]).astype(BF16)
        for j in range(some):
            at = pl.ds(pl.multiple_of((i * some + j) * PAIR, PAIR), PAIR)
            for chip in range(chips):
                part = dealt[chip * PAIR : (chip + 1) * PAIR, j * bins : (j + 1) * bins]
                out[chip, at, :] = part
        return carry

    lax.fori_loop(0, planes // some, deal, 0, unroll=4)

    body = planes * PAIR
    aim_row = target(iota((chips, both), 0))
    lane = iota((bins, both), 0)
    codes = jnp.zeros((chips, bins), F32)
    for kind, (shift, z) in enumerate(((0, None), (-1, planes - 1), (1, 0))):
        picked = ((slab == aim_row + shift).astype(F32) * code).astype(BF16)
        codes = codes + matmul(picked, one_hot(slot + kind * PAIR == lane), (1, 1))
        if kind:
            edge = one_hot((slab == aim + shift) & here)
            dealt = matmul(edge, flat[:, z * bins : (z + 1) * bins]).astype(BF16)
            at = body + (kind - 1) * PAIR
            for chip in range(chips):
                out[chip, at : at + PAIR, :] = dealt[chip * PAIR : (chip + 1) * PAIR, :]
    codes = codes.astype(BF16)
    for chip in range(chips):
        spread = jnp.broadcast_to(codes[chip : chip + 1, :].astype(F32), (META, bins))
        out[chip, body + 2 * PAIR :, :] = spread.astype(BF16)


def bucket(raws, tables, chips, relative, planes, lines):
    rows, bins = raws[0].shape
    sent = (planes + 2) * PAIR + META
    return pl.pallas_call(
        functools.partial(bucket_kernel, chips, relative, planes, lines),
        out_shape=jax.ShapeDtypeStruct((chips, sent, bins), BF16),
        in_specs=[SPEC_VMEM] * 4,
        out_specs=SPEC_VMEM,
        scratch_shapes=[VMEM((2, rows, bins), F32), VMEM((2 * rows // planes, planes * bins), BF16)],
        compiler_params=params(24),
        cost_estimate=cost(10**8, 4 * MIB),
        name="bucket",
    )(*raws, *tables)


def relay_kernel(count, unread, *refs):
    arrived, out = refs[:count], refs[count + unread]
    for i, ref in enumerate(arrived):
        out[i] = ref[0]


def relay(arrived, passed, after):
    count = len(arrived)
    like = [jax.ShapeDtypeStruct(value.shape, value.dtype) for value in passed]
    joined, *rest = pl.pallas_call(
        functools.partial(relay_kernel, count, len(passed) + len(after)),
        out_shape=[jax.ShapeDtypeStruct((count, *arrived[0].shape[1:]), BF16), *like],
        in_specs=[SPEC_VMEM] * count + [SPEC_ANY] * (len(passed) + len(after)),
        out_specs=[SPEC_VMEM] + [SPEC_ANY] * len(passed),
        input_output_aliases={count + i: 1 + i for i in range(len(passed))},
        compiler_params=params(8),
        cost_estimate=cost(0, MIB),
        name="relay",
    )(*arrived, *passed, *after)
    return joined, rest


def behind_kernel(*refs):
    del refs


def behind(passed, after):
    return pl.pallas_call(
        behind_kernel,
        out_shape=[jax.ShapeDtypeStruct(value.shape, value.dtype) for value in passed],
        in_specs=[SPEC_ANY] * (len(passed) + 1),
        out_specs=[SPEC_ANY] * len(passed),
        input_output_aliases={i: i for i in range(len(passed))},
        compiler_params=params(8),
        cost_estimate=cost(0, 0),
        name="behind",
    )(*passed, after)


def mix(w, here, down, up):
    return ((1.0 - 2.0 * w) * here + w * (down + up)).astype(BF16)


def blur_kernel(lines, width, activity, *refs):
    blurred, low_out, high_out = refs[-3:]
    rows, length = activity.shape
    planes = rows // lines
    edge = 2 * lines
    low_out[0:edge, :] = activity[rows - edge :, :]
    low_out[edge : edge + 8, :] = jnp.full((8, length), width[planes - 1], F32)
    high_out[0:edge, :] = activity[0:edge, :]
    high_out[edge : edge + 8, :] = jnp.full((8, length), width[0], F32)

    def inner(z, carry):
        start = pl.multiple_of(z * lines, lines)
        here = activity[pl.ds(start, lines), :]
        down = activity[pl.ds(pl.multiple_of(start - lines, lines), lines), :]
        up = activity[pl.ds(pl.multiple_of(start + lines, lines), lines), :]
        at = pl.ds(pl.multiple_of(start - lines, lines), lines)
        blurred[at, :] = mix(width[z], here, down, up)
        return carry

    lax.fori_loop(1, planes - 1, inner, 0)


def blur(width, activity, after, lines):
    rows, length = activity.shape
    shape = jax.ShapeDtypeStruct((2 * lines + 8, length), F32)
    return pl.pallas_call(
        functools.partial(blur_kernel, lines),
        out_shape=(jax.ShapeDtypeStruct((rows - 2 * lines, length), BF16), shape, shape),
        in_specs=[SPEC_SMEM, SPEC_VMEM] + [SPEC_ANY] * len(after),
        out_specs=(SPEC_VMEM, SPEC_VMEM, SPEC_VMEM),
        compiler_params=params(12),
        cost_estimate=cost(0, 4 * MIB),
        name="blur",
    )(width, activity, *after)


def edge_kernel(lines, groups, after, width, low, high, activity, sensitivity, *refs):
    kernels, refs = refs[:groups], refs[groups + after :]
    edges, gain, blurred = refs[:groups], refs[groups], refs[groups + 1]
    rows, length = activity.shape
    planes = rows // lines
    bins = 256

    def plane(z):
        return activity[z * lines : (z + 1) * lines, :]

    near_low, near_high = low[lines : 2 * lines, :], high[0:lines, :]
    wide_low = low[2 * lines : 2 * lines + 1, :]
    wide_high = high[2 * lines : 2 * lines + 1, :]
    final, before = plane(planes - 1), plane(planes - 2)
    blurred[0:lines, :] = mix(wide_low, near_low, low[0:lines, :], plane(0))
    blurred[lines : 2 * lines, :] = mix(width[0], plane(0), near_low, plane(1))
    blurred[2 * lines : 3 * lines, :] = mix(width[planes - 1], final, before, near_high)
    blurred[3 * lines : 4 * lines, :] = mix(wide_high, near_high, final, high[lines : 2 * lines, :])
    for kernel, edge in zip(kernels, edges):

        def project(i, carry, kernel=kernel, edge=edge):
            columns = pl.ds(pl.multiple_of(i * bins, bins), bins)
            estimate = matmul(blurred[...], kernel[columns, :], (1, 1))
            edge[:, columns] = 1.0 / (estimate + BACKGROUND)
            return carry

        lax.fori_loop(0, kernel.shape[0] // bins, project, 0)

    def divide(i, carry):
        at = pl.ds(pl.multiple_of(i * lines, lines), lines)
        gain[at, :] = activity[at, :] / sensitivity[at, :]
        return carry

    lax.fori_loop(0, planes, divide, 0)


def edge(width, low, high, activity, sensitivity, kernels, after, lines):
    rows, length = activity.shape
    groups = len(kernels)
    shape = jax.ShapeDtypeStruct((4 * lines, kernels[0].shape[0]), F32)
    *edges, gain = pl.pallas_call(
        functools.partial(edge_kernel, lines, groups, len(after)),
        out_shape=[shape] * groups + [jax.ShapeDtypeStruct((rows, length), F32)],
        in_specs=[SPEC_SMEM] + [SPEC_VMEM] * (4 + groups) + [SPEC_ANY] * len(after),
        out_specs=[SPEC_VMEM] * (groups + 1),
        scratch_shapes=[VMEM((4 * lines, length), BF16)],
        compiler_params=params(LIMIT_BACK),
        cost_estimate=cost(groups * 2 * 4 * lines * length * 1024, 12 * MIB),
        name="edge",
    )(width, low, high, activity, sensitivity, *kernels, *after)
    return edges, gain


def front_kernel(after, spacing, offset, blurred, *refs):
    k_out, r_out = refs[after:]
    length = blurred.shape[1]
    angles = spacing.shape[0]
    bins = k_out.shape[0] // angles
    step_width = length / bins
    deviation = 0.25 * step_width
    scale = 1.0 / (deviation * math.sqrt(2.0 * math.pi))
    sharp = -math.log2(math.e) / (2.0 * deviation * deviation)
    some = 32
    pair = 4
    voxel = iota((1, length), 1).astype(F32) + 0.5 - length / 2
    bin_at = iota((some, 1), 0).astype(F32) + 0.5 - bins / 2

    def group(q, carry):
        begin = pl.multiple_of(q * pair * bins, pair * bins)
        for i in range(pair * bins // some):
            a = q * pair + i * some // bins
            centre = (bin_at + float(i * some % bins)) * spacing[a] + offset[a]
            distance = voxel - centre
            value = jnp.exp2(distance * distance * sharp) * scale
            k_out[pl.ds(begin + i * some, some), :] = value.astype(BF16)
        columns = pl.ds(begin, pair * bins)
        estimate = matmul(blurred[...], k_out[columns, :], (1, 1))
        r_out[:, columns] = 1.0 / (estimate + BACKGROUND)
        return carry

    lax.fori_loop(0, angles // pair, group, 0)


def front(spacing, offset, blurred, bins, after=()):
    (angles,) = spacing.shape
    wide = angles * bins
    rows, length = blurred.shape
    return pl.pallas_call(
        functools.partial(front_kernel, len(after)),
        out_shape=(
            jax.ShapeDtypeStruct((wide, length), BF16),
            jax.ShapeDtypeStruct((rows, wide), F32),
        ),
        in_specs=[SPEC_SMEM, SPEC_SMEM, SPEC_VMEM] + [SPEC_ANY] * len(after),
        out_specs=(SPEC_VMEM, SPEC_VMEM),
        compiler_params=params(LIMIT_FRONT),
        cost_estimate=cost(2 * rows * length * wide, 8 * MIB),
        name="front",
    )(spacing, offset, blurred, *after)


def back_kernel(counts, has_prior, last, lines, *refs):
    refs = list(refs)

    def take(number):
        taken = refs[:number]
        del refs[:number]
        return taken

    received = take(len(counts))
    k_buf, r_buf, edge_buf = take(3)
    (prior,) = take(1) if has_prior else (None,)
    if last:
        width, low, high, gain = take(4)
    (out,) = take(1)
    (rounded,) = take(1)
    if last:
        total, updated, sems = take(3)
    sources = [(ref, s) for ref, count in zip(received, counts) for s in range(count)]
    bins = received[0].shape[-1]
    extended, wide = rounded.shape
    length = k_buf.shape[1]
    angles = wide // bins
    planes = extended // lines - 2
    body = planes * PAIR
    group = bins // PAIR

    rows = [
        ref[s, body + 2 * PAIR : body + 2 * PAIR + META, :].astype(F32)[0:8, :] for ref, s in sources
    ]
    lane = iota((8, bins), 1)
    named = []
    for kind in range(3):
        parts = []
        for first in range(0, len(rows), group):
            codes = jnp.zeros((8, bins), F32)
            for i in range(first, min(first + group, len(rows))):
                own = jnp.where(lane // PAIR == kind, rows[i], 0.0)
                codes = codes + pltpu.roll(own, (i - first - kind) % group * PAIR, 1)
            parts.append(codes[0:1, :])
        codes = jnp.concatenate(parts, axis=1).astype(I32)
        named.append(one_hot(codes - 1 == iota((angles * lines, codes.shape[1]), 0)))

    def sums(kind, at, start, inverse, first):
        held = [ref[s, pl.ds(at, PAIR), :] for ref, s in sources]
        spare = -len(held) % group * PAIR
        if spare:
            held.append(jnp.zeros((spare, bins), BF16))
        sums = matmul(named[kind], jnp.concatenate(held))
        for a in range(angles):
            columns = pl.ds(a * bins, bins)
            ratio = sums[a * lines : (a + 1) * lines, :] * inverse[pl.ds(first, lines), columns]
            rounded[pl.ds(start, lines), columns] = ratio.astype(BF16)

    sums(1, body, 0, edge_buf, 0)
    sums(0, 0, lines, edge_buf, lines)
    sums(0, body - PAIR, extended - 2 * lines, edge_buf, 2 * lines)
    sums(2, body + PAIR, extended - lines, edge_buf, 3 * lines)

    def inner(z, carry):
        start = pl.multiple_of(z * lines, lines)
        first = pl.multiple_of(start - lines, lines)
        sums(0, pl.multiple_of(z * PAIR, PAIR), start + lines, r_buf, first)
        return carry

    lax.fori_loop(1, planes - 1, inner, 0, unroll=5)

    block = total.shape[2] if last else 512
    steps = length // block

    def project(columns):
        value = matmul(rounded[...], k_buf[:, columns])
        return prior[:, columns] + value if has_prior else value

    if not last:

        def step(i, carry):
            columns = pl.ds(pl.multiple_of(i * block, block), block)
            out[:, columns] = project(columns)
            return carry

        lax.fori_loop(0, steps, step, 0)
        return

    def write(i):
        columns = pl.ds(i * block, block)
        return pltpu.make_async_copy(updated.at[i % 2], out.at[:, columns], sems.at[i % 2])

    def smooth(i):
        held, columns = total.at[i % 2], pl.ds(i * block, block)
        for z in range(planes):
            edge_low = low[2 * lines : 2 * lines + 1, 0:block] if z == 0 else width[z - 1]
            edge_high = high[2 * lines : 2 * lines + 1, 0:block] if z == planes - 1 else width[z + 1]
            start = z * lines
            down = held[start : start + lines, :]
            here = held[start + lines : start + 2 * lines, :]
            up = held[start + 2 * lines : start + 3 * lines, :]
            value = (1.0 - 2.0 * width[z]) * here + edge_low * down + edge_high * up
            at = pl.ds(start, lines)
            updated[i % 2, at, :] = value * gain[at, columns]

    for i in range(steps + 1):
        if i >= 3:
            write(i - 3).wait()
        if i < steps:
            total[i % 2] = project(pl.ds(i * block, block))
        if i:
            smooth(i - 1)
            write(i - 1).start()
    for i in range(max(0, steps - 2), steps):
        write(i).wait()


def back(pieces, k, r, edges, prior, final, lines):
    rows, wide = r.shape
    extended = rows + 4 * lines
    _, length = k.shape
    operands = [*pieces, k, r, edges]
    specs = [SPEC_VMEM] * len(operands)
    if prior is not None:
        operands.append(prior)
        specs.append(SPEC_VMEM)
    scratch = [VMEM((extended, wide), BF16)]
    shape = (extended, length)
    if final is not None:
        rows = extended - 2 * lines
        operands += final
        specs += [SPEC_SMEM] + [SPEC_VMEM] * 3
        scratch += [
            VMEM((2, extended, BLOCK), F32),
            VMEM((2, rows, BLOCK), F32),
            pltpu.SemaphoreType.DMA((2,)),
        ]
        shape = (rows, length)
    return pl.pallas_call(
        functools.partial(
            back_kernel,
            [piece.shape[0] for piece in pieces],
            prior is not None,
            final is not None,
            lines,
        ),
        out_shape=jax.ShapeDtypeStruct(shape, F32),
        in_specs=specs,
        out_specs=SPEC_VMEM if final is None else SPEC_HBM,
        scratch_shapes=scratch,
        compiler_params=params(LIMIT_BACK if final is None else LIMIT_UPDATE),
        cost_estimate=cost(2 * extended * length * wide, 12 * MIB),
        name="back" if final is None else "update",
    )(*operands)


def swap(value):
    return lax.ppermute(value, "view", [(0, 1), (1, 0)])


def flip(value, mask):
    size = lax.axis_size("slab")
    return lax.ppermute(value, "slab", [(i, i ^ mask) for i in range(size)])


def on_device(
    activity, sensitivity, psf_width, measured, block_slab, block_line, block_angle, subset_views
):
    planes, lines, length = activity.shape
    _, blocks, _, bins = measured.shape
    slabs, view_count = lax.axis_size("slab"), lax.axis_size("view")
    assert 2 * blocks <= SLOTS * slabs and 2 * blocks == bins and slabs <= WIDE
    assert subset_views.shape[1] * lines <= 256

    flat = activity.reshape(planes * lines, length)
    raw = measured.reshape(blocks * planes, bins)
    parts = [block_slab.reshape(1, blocks), block_line, block_angle]
    parts = [jnp.pad(part, ((i, 7 - i), (0, bins - blocks))) for i, part in enumerate(parts)]
    table = functools.reduce(jnp.add, parts)
    raws, tables = [raw, flip(raw, 1)], [table, flip(table, 1)]
    ups = [(i, i + 1) for i in range(slabs - 1)]
    downs = [(j, i) for i, j in ups]
    chips = slabs // 2
    step_width = length / bins

    def forward(view, blurred, behind=()):
        angle = math.pi * view.astype(F32) / VIEWS_ALL
        spacing = step_width * (0.75 + 0.25 * jnp.cos(2.0 * angle))
        offset = 1.5 * step_width * jnp.sin(angle)
        return front(spacing, offset, blurred, bins, behind)

    if slabs == 16 and view_count == 2:
        other = swap(subset_views)
        send = bucket(raws, tables, chips, True, planes, lines)
        blurred, *mine = blur(psf_width, flat, [send, other], lines)
        near = [send[0:1]] + [flip(send[j : j + 1], 2 * j) for j in range(1, 4)]
        far = [flip(send[j : j + 1], 2 * j) for j in (4, 5)]
        fronts = [forward(subset_views[0], blurred)]
        joined, passed = relay(near, [send[6:7], send[7:8]], [fronts[0][0]])
        far += [flip(passed[0], 12), flip(passed[1], 14)]
        over = [swap(joined)] + [swap(jnp.concatenate(part)) for part in (far[:2], far[2:])]
        pieces = [[joined, *far], over]
        fronts.append(forward(other[0], blurred, [joined]))
        mine = behind(mine, fronts[1][0])
        behind_edge = [over[0]]
    else:
        send = bucket(raws, tables, chips, False, planes, lines)
        blurred, *mine = blur(psf_width, flat, [send], lines)
        cores = [[2 * chip + core for chip in range(chips)] for core in range(2)]
        own = lax.all_to_all(
            send, "slab", split_axis=0, concat_axis=0, axis_index_groups=cores, tiled=True
        )
        everyone = lax.all_gather(own, "view")
        pieces = [[everyone[g]] for g in range(view_count)]
        gathered = lax.all_gather(subset_views[0], "view")
        fronts = [forward(gathered[g], blurred) for g in range(view_count)]
        behind_edge = []

    low = lax.ppermute(mine[0], "slab", ups)
    high = lax.ppermute(mine[1], "slab", downs)
    kernels, inverses = zip(*fronts)
    whole = sensitivity.reshape(planes * lines, length)
    edges, gain = edge(psf_width, low, high, flat, whole, kernels, behind_edge, lines)

    result = None
    for g in range(view_count):
        final = None
        if g == view_count - 1:
            final = [psf_width, low, high, gain]
        result = back(pieces[g], kernels[g], inverses[g], edges[g], result, final, lines)
    return result.reshape(planes, lines, length)


def solution(mesh):
    in_specs = (
        P("slab", None, None),
        P("slab", None, None),
        P("slab"),
        P("view", "slab", None, None),
        P("view", "slab", None),
        P("view", "slab"),
        P("view", "slab"),
        P("view", None),
    )
    out_specs = P("slab", None, None)
    return jax.shard_map(
        on_device, mesh=mesh, in_specs=in_specs, out_specs=out_specs, check_vma=False
    )
```

```python
import functools
import math

import jax
import jax.numpy as jnp
from jax import lax
from jax.experimental import pallas as pl
from jax.experimental.pallas import tpu as pltpu
from jax.sharding import PartitionSpec as P

VIEWS_ALL = 336
BACKGROUND = 0.05
SLOTS = 8
PAIR = 2 * SLOTS
META = 16
WIDE = 64
F32 = jnp.float32
BF16 = jnp.bfloat16
I32 = jnp.int32
SMEM = pltpu.SMEM
VMEM = pltpu.VMEM
MIB = 1024 * 1024
BLOCK = 512
LIMIT_FRONT = 12
LIMIT_BACK = 14
LIMIT_UPDATE = 20


def iota(shape, dim):
    return lax.broadcasted_iota(I32, shape, dim)


def matmul(a, b, contract=(1, 0)):
    dims = (((contract[0],), (contract[1],)), ((), ()))
    return lax.dot_general(a, b, dims, preferred_element_type=F32)


def params(limit):
    return pltpu.CompilerParams(vmem_limit_bytes=limit * MIB)


def cost(flops, moved):
    del flops, moved
    return pl.CostEstimate(flops=0, bytes_accessed=0, transcendentals=0)


SPEC_SMEM = pl.BlockSpec(memory_space=SMEM)
SPEC_VMEM = pl.BlockSpec(memory_space=VMEM)
SPEC_ANY = pl.BlockSpec(memory_space=pl.ANY)
SPEC_HBM = pl.BlockSpec(memory_space=pltpu.HBM)


def one_hot(mask):
    return mask.astype(F32).astype(BF16)


def bucket_kernel(chips, relative, planes, lines, *refs):
    raws, tables = refs[0:2], refs[2:4]
    out, wide, flat = refs[4:]
    rows, bins = raws[0].shape
    blocks = rows // planes
    both = 2 * blocks
    me = lax.axis_index("slab")

    for i, raw in enumerate(raws):
        wide[i] = raw[...].astype(F32)

    def turn(z, carry):
        column = pl.ds(pl.multiple_of(z * bins, bins), bins)
        for i in range(2):
            part = wide[i, pl.ds(z, blocks, stride=planes), :]
            flat[i * blocks : (i + 1) * blocks, column] = part.astype(BF16)
        return carry

    lax.fori_loop(0, planes, turn, 0, unroll=4)

    def lanes(row):
        return tables[0][row : row + 1, :] + pltpu.roll(tables[1][row : row + 1, :], blocks, 1)

    slab, code = lanes(0), (lanes(2) * lines + lanes(1) + 1).astype(F32)
    shape = (both, both)
    earlier = (iota(shape, 0) < iota(shape, 1)) & (iota(shape, 0) // blocks == iota(shape, 1) // blocks)
    names = (iota((WIDE, both), 0) == slab).astype(F32)
    ranks = matmul(names.astype(BF16), one_hot(earlier))
    slot = jnp.sum(names * ranks, axis=0, keepdims=True).astype(I32)
    slot = slot + iota((1, both), 1) // blocks * SLOTS

    def target(chip):
        return (2 * chip) ^ me if relative else 2 * chip + (me & 1)

    row = iota((chips * PAIR, both), 0)
    aim = target(row // PAIR)
    here = slot == row % PAIR
    chosen = one_hot((slab == aim) & here)

    some = 2

    def deal(i, carry):
        column = pl.ds(pl.multiple_of(i * some * bins, some * bins), some * bins)
        dealt = matmul(chosen, flat[:, column]).astype(BF16)
        for j in range(some):
            at = pl.ds(pl.multiple_of((i * some + j) * PAIR, PAIR), PAIR)
            for chip in range(chips):
                part = dealt[chip * PAIR : (chip + 1) * PAIR, j * bins : (j + 1) * bins]
                out[chip, at, :] = part
        return carry

    lax.fori_loop(0, planes // some, deal, 0, unroll=4)

    body = planes * PAIR
    aim_row = target(iota((chips, both), 0))
    lane = iota((bins, both), 0)
    codes = jnp.zeros((chips, bins), F32)
    for kind, (shift, z) in enumerate(((0, None), (-1, planes - 1), (1, 0))):
        picked = ((slab == aim_row + shift).astype(F32) * code).astype(BF16)
        codes = codes + matmul(picked, one_hot(slot + kind * PAIR == lane), (1, 1))
        if kind:
            edge = one_hot((slab == aim + shift) & here)
            dealt = matmul(edge, flat[:, z * bins : (z + 1) * bins]).astype(BF16)
            at = body + (kind - 1) * PAIR
            for chip in range(chips):
                out[chip, at : at + PAIR, :] = dealt[chip * PAIR : (chip + 1) * PAIR, :]
    codes = codes.astype(BF16)
    for chip in range(chips):
        spread = jnp.broadcast_to(codes[chip : chip + 1, :].astype(F32), (META, bins))
        out[chip, body + 2 * PAIR :, :] = spread.astype(BF16)


def bucket(raws, tables, chips, relative, planes, lines):
    rows, bins = raws[0].shape
    sent = (planes + 2) * PAIR + META
    return pl.pallas_call(
        functools.partial(bucket_kernel, chips, relative, planes, lines),
        out_shape=jax.ShapeDtypeStruct((chips, sent, bins), BF16),
        in_specs=[SPEC_VMEM] * 4,
        out_specs=SPEC_VMEM,
        scratch_shapes=[VMEM((2, rows, bins), F32), VMEM((2 * rows // planes, planes * bins), BF16)],
        compiler_params=params(24),
        cost_estimate=cost(10**8, 4 * MIB),
        name="bucket",
    )(*raws, *tables)


def relay_kernel(count, unread, *refs):
    arrived, out = refs[:count], refs[count + unread]
    for i, ref in enumerate(arrived):
        out[i] = ref[0]


def relay(arrived, passed, after):
    count = len(arrived)
    like = [jax.ShapeDtypeStruct(value.shape, value.dtype) for value in passed]
    joined, *rest = pl.pallas_call(
        functools.partial(relay_kernel, count, len(passed) + len(after)),
        out_shape=[jax.ShapeDtypeStruct((count, *arrived[0].shape[1:]), BF16), *like],
        in_specs=[SPEC_VMEM] * count + [SPEC_ANY] * (len(passed) + len(after)),
        out_specs=[SPEC_VMEM] + [SPEC_ANY] * len(passed),
        input_output_aliases={count + i: 1 + i for i in range(len(passed))},
        compiler_params=params(8),
        cost_estimate=cost(0, MIB),
        name="relay",
    )(*arrived, *passed, *after)
    return joined, rest


def behind_kernel(*refs):
    del refs


def behind(passed, after):
    return pl.pallas_call(
        behind_kernel,
        out_shape=[jax.ShapeDtypeStruct(value.shape, value.dtype) for value in passed],
        in_specs=[SPEC_ANY] * (len(passed) + 1),
        out_specs=[SPEC_ANY] * len(passed),
        input_output_aliases={i: i for i in range(len(passed))},
        compiler_params=params(8),
        cost_estimate=cost(0, 0),
        name="behind",
    )(*passed, after)


def mix(w, here, down, up):
    return ((1.0 - 2.0 * w) * here + w * (down + up)).astype(BF16)


def blur_kernel(lines, width, activity, *refs):
    blurred, low_out, high_out = refs[-3:]
    rows, length = activity.shape
    planes = rows // lines
    edge = 2 * lines
    low_out[0:edge, :] = activity[rows - edge :, :]
    low_out[edge : edge + 8, :] = jnp.full((8, length), width[planes - 1], F32)
    high_out[0:edge, :] = activity[0:edge, :]
    high_out[edge : edge + 8, :] = jnp.full((8, length), width[0], F32)

    def inner(z, carry):
        start = pl.multiple_of(z * lines, lines)
        here = activity[pl.ds(start, lines), :]
        down = activity[pl.ds(pl.multiple_of(start - lines, lines), lines), :]
        up = activity[pl.ds(pl.multiple_of(start + lines, lines), lines), :]
        at = pl.ds(pl.multiple_of(start - lines, lines), lines)
        blurred[at, :] = mix(width[z], here, down, up)
        return carry

    lax.fori_loop(1, planes - 1, inner, 0)


def blur(width, activity, after, lines):
    rows, length = activity.shape
    shape = jax.ShapeDtypeStruct((2 * lines + 8, length), F32)
    return pl.pallas_call(
        functools.partial(blur_kernel, lines),
        out_shape=(jax.ShapeDtypeStruct((rows - 2 * lines, length), BF16), shape, shape),
        in_specs=[SPEC_SMEM, SPEC_VMEM] + [SPEC_ANY] * len(after),
        out_specs=(SPEC_VMEM, SPEC_VMEM, SPEC_VMEM),
        compiler_params=params(12),
        cost_estimate=cost(0, 4 * MIB),
        name="blur",
    )(width, activity, *after)


def edge_kernel(lines, groups, after, width, low, high, activity, sensitivity, *refs):
    kernels, refs = refs[:groups], refs[groups + after :]
    edges, gain, blurred = refs[:groups], refs[groups], refs[groups + 1]
    rows, length = activity.shape
    planes = rows // lines
    bins = 256

    def plane(z):
        return activity[z * lines : (z + 1) * lines, :]

    near_low, near_high = low[lines : 2 * lines, :], high[0:lines, :]
    wide_low = low[2 * lines : 2 * lines + 1, :]
    wide_high = high[2 * lines : 2 * lines + 1, :]
    final, before = plane(planes - 1), plane(planes - 2)
    blurred[0:lines, :] = mix(wide_low, near_low, low[0:lines, :], plane(0))
    blurred[lines : 2 * lines, :] = mix(width[0], plane(0), near_low, plane(1))
    blurred[2 * lines : 3 * lines, :] = mix(width[planes - 1], final, before, near_high)
    blurred[3 * lines : 4 * lines, :] = mix(wide_high, near_high, final, high[lines : 2 * lines, :])
    for kernel, edge in zip(kernels, edges):

        def project(i, carry, kernel=kernel, edge=edge):
            columns = pl.ds(pl.multiple_of(i * bins, bins), bins)
            estimate = matmul(blurred[...], kernel[columns, :], (1, 1))
            edge[:, columns] = 1.0 / (estimate + BACKGROUND)
            return carry

        lax.fori_loop(0, kernel.shape[0] // bins, project, 0)

    def divide(i, carry):
        at = pl.ds(pl.multiple_of(i * lines, lines), lines)
        gain[at, :] = activity[at, :] / sensitivity[at, :]
        return carry

    lax.fori_loop(0, planes, divide, 0)


def edge(width, low, high, activity, sensitivity, kernels, after, lines):
    rows, length = activity.shape
    groups = len(kernels)
    shape = jax.ShapeDtypeStruct((4 * lines, kernels[0].shape[0]), F32)
    *edges, gain = pl.pallas_call(
        functools.partial(edge_kernel, lines, groups, len(after)),
        out_shape=[shape] * groups + [jax.ShapeDtypeStruct((rows, length), F32)],
        in_specs=[SPEC_SMEM] + [SPEC_VMEM] * (4 + groups) + [SPEC_ANY] * len(after),
        out_specs=[SPEC_VMEM] * (groups + 1),
        scratch_shapes=[VMEM((4 * lines, length), BF16)],
        compiler_params=params(LIMIT_BACK),
        cost_estimate=cost(groups * 2 * 4 * lines * length * 1024, 12 * MIB),
        name="edge",
    )(width, low, high, activity, sensitivity, *kernels, *after)
    return edges, gain


def front_kernel(after, spacing, offset, blurred, *refs):
    k_out, r_out = refs[after:]
    length = blurred.shape[1]
    angles = spacing.shape[0]
    bins = k_out.shape[0] // angles
    step_width = length / bins
    deviation = 0.25 * step_width
    scale = 1.0 / (deviation * math.sqrt(2.0 * math.pi))
    sharp = -math.log2(math.e) / (2.0 * deviation * deviation)
    some = 32
    pair = 4
    voxel = iota((1, length), 1).astype(F32) + 0.5 - length / 2
    bin_at = iota((some, 1), 0).astype(F32) + 0.5 - bins / 2

    def group(q, carry):
        begin = pl.multiple_of(q * pair * bins, pair * bins)
        for i in range(pair * bins // some):
            a = q * pair + i * some // bins
            centre = (bin_at + float(i * some % bins)) * spacing[a] + offset[a]
            distance = voxel - centre
            value = jnp.exp2(distance * distance * sharp) * scale
            k_out[pl.ds(begin + i * some, some), :] = value.astype(BF16)
        columns = pl.ds(begin, pair * bins)
        estimate = matmul(blurred[...], k_out[columns, :], (1, 1))
        r_out[:, columns] = 1.0 / (estimate + BACKGROUND)
        return carry

    lax.fori_loop(0, angles // pair, group, 0)


def front(spacing, offset, blurred, bins, after=()):
    (angles,) = spacing.shape
    wide = angles * bins
    rows, length = blurred.shape
    return pl.pallas_call(
        functools.partial(front_kernel, len(after)),
        out_shape=(
            jax.ShapeDtypeStruct((wide, length), BF16),
            jax.ShapeDtypeStruct((rows, wide), F32),
        ),
        in_specs=[SPEC_SMEM, SPEC_SMEM, SPEC_VMEM] + [SPEC_ANY] * len(after),
        out_specs=(SPEC_VMEM, SPEC_VMEM),
        compiler_params=params(LIMIT_FRONT),
        cost_estimate=cost(2 * rows * length * wide, 8 * MIB),
        name="front",
    )(spacing, offset, blurred, *after)


def back_kernel(counts, has_prior, last, lines, *refs):
    refs = list(refs)

    def take(number):
        taken = refs[:number]
        del refs[:number]
        return taken

    received = take(len(counts))
    k_buf, r_buf, edge_buf = take(3)
    (prior,) = take(1) if has_prior else (None,)
    if last:
        width, low, high, gain = take(4)
    (out,) = take(1)
    (rounded,) = take(1)
    if last:
        total, updated, sems = take(3)
    sources = [(ref, s) for ref, count in zip(received, counts) for s in range(count)]
    bins = received[0].shape[-1]
    extended, wide = rounded.shape
    length = k_buf.shape[1]
    angles = wide // bins
    planes = extended // lines - 2
    body = planes * PAIR
    group = bins // PAIR

    rows = [
        ref[s, body + 2 * PAIR : body + 2 * PAIR + META, :].astype(F32)[0:8, :] for ref, s in sources
    ]
    lane = iota((8, bins), 1)
    named = []
    for kind in range(3):
        parts = []
        for first in range(0, len(rows), group):
            codes = jnp.zeros((8, bins), F32)
            for i in range(first, min(first + group, len(rows))):
                own = jnp.where(lane // PAIR == kind, rows[i], 0.0)
                codes = codes + pltpu.roll(own, (i - first - kind) % group * PAIR, 1)
            parts.append(codes[0:1, :])
        codes = jnp.concatenate(parts, axis=1).astype(I32)
        named.append(one_hot(codes - 1 == iota((angles * lines, codes.shape[1]), 0)))

    def sums(kind, at, start, inverse, first):
        held = [ref[s, pl.ds(at, PAIR), :] for ref, s in sources]
        spare = -len(held) % group * PAIR
        if spare:
            held.append(jnp.zeros((spare, bins), BF16))
        sums = matmul(named[kind], jnp.concatenate(held))
        for a in range(angles):
            columns = pl.ds(a * bins, bins)
            ratio = sums[a * lines : (a + 1) * lines, :] * inverse[pl.ds(first, lines), columns]
            rounded[pl.ds(start, lines), columns] = ratio.astype(BF16)

    sums(1, body, 0, edge_buf, 0)
    sums(0, 0, lines, edge_buf, lines)
    sums(0, body - PAIR, extended - 2 * lines, edge_buf, 2 * lines)
    sums(2, body + PAIR, extended - lines, edge_buf, 3 * lines)

    def inner(z, carry):
        start = pl.multiple_of(z * lines, lines)
        first = pl.multiple_of(start - lines, lines)
        sums(0, pl.multiple_of(z * PAIR, PAIR), start + lines, r_buf, first)
        return carry

    lax.fori_loop(1, planes - 1, inner, 0, unroll=5)

    block = total.shape[2] if last else 512
    steps = length // block

    def project(columns):
        value = matmul(rounded[...], k_buf[:, columns])
        return prior[:, columns] + value if has_prior else value

    if not last:

        def step(i, carry):
            columns = pl.ds(pl.multiple_of(i * block, block), block)
            out[:, columns] = project(columns)
            return carry

        lax.fori_loop(0, steps, step, 0)
        return

    def write(i):
        columns = pl.ds(i * block, block)
        return pltpu.make_async_copy(updated.at[i % 2], out.at[:, columns], sems.at[i % 2])

    def smooth(i):
        held, columns = total.at[i % 2], pl.ds(i * block, block)
        for z in range(planes):
            edge_low = low[2 * lines : 2 * lines + 1, 0:block] if z == 0 else width[z - 1]
            edge_high = high[2 * lines : 2 * lines + 1, 0:block] if z == planes - 1 else width[z + 1]
            start = z * lines
            down = held[start : start + lines, :]
            here = held[start + lines : start + 2 * lines, :]
            up = held[start + 2 * lines : start + 3 * lines, :]
            value = (1.0 - 2.0 * width[z]) * here + edge_low * down + edge_high * up
            at = pl.ds(start, lines)
            updated[i % 2, at, :] = value * gain[at, columns]

    for i in range(steps + 1):
        if i >= 3:
            write(i - 3).wait()
        if i < steps:
            total[i % 2] = project(pl.ds(i * block, block))
        if i:
            smooth(i - 1)
            write(i - 1).start()
    for i in range(max(0, steps - 2), steps):
        write(i).wait()


def back(pieces, k, r, edges, prior, final, lines):
    rows, wide = r.shape
    extended = rows + 4 * lines
    _, length = k.shape
    operands = [*pieces, k, r, edges]
    specs = [SPEC_VMEM] * len(operands)
    if prior is not None:
        operands.append(prior)
        specs.append(SPEC_VMEM)
    scratch = [VMEM((extended, wide), BF16)]
    shape = (extended, length)
    if final is not None:
        rows = extended - 2 * lines
        operands += final
        specs += [SPEC_SMEM] + [SPEC_VMEM] * 3
        scratch += [
            VMEM((2, extended, BLOCK), F32),
            VMEM((2, rows, BLOCK), F32),
            pltpu.SemaphoreType.DMA((2,)),
        ]
        shape = (rows, length)
    return pl.pallas_call(
        functools.partial(
            back_kernel,
            [piece.shape[0] for piece in pieces],
            prior is not None,
            final is not None,
            lines,
        ),
        out_shape=jax.ShapeDtypeStruct(shape, F32),
        in_specs=specs,
        out_specs=SPEC_VMEM if final is None else SPEC_HBM,
        scratch_shapes=scratch,
        compiler_params=params(LIMIT_BACK if final is None else LIMIT_UPDATE),
        cost_estimate=cost(2 * extended * length * wide, 12 * MIB),
        name="back" if final is None else "update",
    )(*operands)


def swap(value):
    return lax.ppermute(value, "view", [(0, 1), (1, 0)])


def flip(value, mask):
    size = lax.axis_size("slab")
    return lax.ppermute(value, "slab", [(i, i ^ mask) for i in range(size)])


def on_device(
    activity, sensitivity, psf_width, measured, block_slab, block_line, block_angle, subset_views
):
    planes, lines, length = activity.shape
    _, blocks, _, bins = measured.shape
    slabs, view_count = lax.axis_size("slab"), lax.axis_size("view")
    assert 2 * blocks <= SLOTS * slabs and 2 * blocks == bins and slabs <= WIDE
    assert subset_views.shape[1] * lines <= 256

    flat = activity.reshape(planes * lines, length)
    raw = measured.reshape(blocks * planes, bins)
    parts = [block_slab.reshape(1, blocks), block_line, block_angle]
    parts = [jnp.pad(part, ((i, 7 - i), (0, bins - blocks))) for i, part in enumerate(parts)]
    table = functools.reduce(jnp.add, parts)
    raws, tables = [raw, flip(raw, 1)], [table, flip(table, 1)]
    ups = [(i, i + 1) for i in range(slabs - 1)]
    downs = [(j, i) for i, j in ups]
    chips = slabs // 2
    step_width = length / bins

    def forward(view, blurred, behind=()):
        angle = math.pi * view.astype(F32) / VIEWS_ALL
        spacing = step_width * (0.75 + 0.25 * jnp.cos(2.0 * angle))
        offset = 1.5 * step_width * jnp.sin(angle)
        return front(spacing, offset, blurred, bins, behind)

    if slabs == 16 and view_count == 2:
        other = swap(subset_views)
        send = bucket(raws, tables, chips, True, planes, lines)
        home = send[0:1]
        home_over = swap(home)
        blurred, *mine = blur(psf_width, flat, [send, other, home_over], lines)
        near = [flip(send[j : j + 1], 2 * j) for j in range(1, 4)]
        far = [flip(send[j : j + 1], 2 * j) for j in (4, 5)]
        fronts = [forward(subset_views[0], blurred)]
        joined, passed = relay(near, [send[6:7], send[7:8]], [fronts[0][0]])
        far += [flip(passed[0], 12), flip(passed[1], 14)]
        over = [swap(joined)] + [swap(jnp.concatenate(part)) for part in (far[:2], far[2:])]
        pieces = [[home, joined, *far], [home_over, *over]]
        fronts.append(forward(other[0], blurred, [joined]))
        mine = behind(mine, fronts[1][0])
        behind_edge = [over[0]]
    else:
        send = bucket(raws, tables, chips, False, planes, lines)
        blurred, *mine = blur(psf_width, flat, [send], lines)
        cores = [[2 * chip + core for chip in range(chips)] for core in range(2)]
        own = lax.all_to_all(
            send, "slab", split_axis=0, concat_axis=0, axis_index_groups=cores, tiled=True
        )
        everyone = lax.all_gather(own, "view")
        pieces = [[everyone[g]] for g in range(view_count)]
        gathered = lax.all_gather(subset_views[0], "view")
        fronts = [forward(gathered[g], blurred) for g in range(view_count)]
        behind_edge = []

    low = lax.ppermute(mine[0], "slab", ups)
    high = lax.ppermute(mine[1], "slab", downs)
    kernels, inverses = zip(*fronts)
    whole = sensitivity.reshape(planes * lines, length)
    edges, gain = edge(psf_width, low, high, flat, whole, kernels, behind_edge, lines)

    result = None
    for g in range(view_count):
        final = None
        if g == view_count - 1:
            final = [psf_width, low, high, gain]
        result = back(pieces[g], kernels[g], inverses[g], edges[g], result, final, lines)
    return result.reshape(planes, lines, length)


def solution(mesh):
    in_specs = (
        P("slab", None, None),
        P("slab", None, None),
        P("slab"),
        P("view", "slab", None, None),
        P("view", "slab", None),
        P("view", "slab"),
        P("view", "slab"),
        P("view", None),
    )
    out_specs = P("slab", None, None)
    return jax.shard_map(
        on_device, mesh=mesh, in_specs=in_specs, out_specs=out_specs, check_vma=False
    )
```
